256 devices in a mesh: view: 8 (over y, core), tm: 16 (over z_lo, x), height: 2 (over z_hi).
Axes of the slice: x: 4, y: 4, z: 8 (z_hi: 2, z_lo: 4; z = z_hi * 4 + z_lo), core: 2. Of those that a mesh axis runs over, the one named last changes fastest.
Arguments:
- query_vectors: bfloat16 [8, 16, 8, 64, 1536], P('view', 'tm', 'height'), may hold values from -120 to 120
- key_vectors: bfloat16 [8, 16, 8, 64, 1536], P('view', 'tm', 'height'), may hold values from -6 to 6
- value_vectors: bfloat16 [8, 16, 8, 64, 1536], P('view', 'tm', 'height'), may hold values from -6 to 6
- out_grad: bfloat16 [8, 16, 8, 64, 1536], P('view', 'tm', 'height'), may hold values from -6 to 6
- epi_rows: int32 [8, 16, 2, 7], P(None, 'tm'), may hold values from 0 to 7
Outputs:
- attended: bfloat16 [8, 16, 8, 64, 1536], P('view', 'tm', 'height')
- query_grad: bfloat16 [8, 16, 8, 64, 1536], P('view', 'tm', 'height')
- key_grad: bfloat16 [8, 16, 8, 64, 1536], P('view', 'tm', 'height')
- value_grad: bfloat16 [8, 16, 8, 64, 1536], P('view', 'tm', 'height')
The draws below stay inside these ranges and needn't reach their ends.
Inputs may be any that keep to these rules, and one draw needn't show every extreme that they name: epi_rows[v, f, b, d - 1] is the row of view (v + d) mod 8 in frame f that holds the epipolar line of query tile b of view v and frame f.
All inputs are finite; a program needn't handle non-finite values.
Results may differ from the reference program's by a relative error of at most 0.0056.
Values may be sent and summed in bfloat16 or wider, within the bound.
A program may use at most 128 MiB of HBM per device.

```python
import jax
import jax.numpy as jnp
from jax import lax

HEADS = 12
HEAD_DIM = 128
FEAT = 1536
TILE_ROWS = 4
COLS = 64
VIEWS = 8
FRAMES = 16
ROWS = 8
N_HEIGHT = 2


def shared_keys(key):
    return jnp.clip(jax.random.normal(key, (VIEWS, FRAMES, ROWS, COLS, HEADS * HEAD_DIM), jnp.float32), -6.0, 6.0)


def draw_key_vectors(key, part):
    base_keys = shared_keys(key)
    return base_keys.astype(jnp.bfloat16)


def draw_query_vectors(key, part):
    base_keys = shared_keys(key)
    key = jax.random.fold_in(key, 5)
    full_shape = base_keys.shape
    fresh = jnp.clip(jax.random.normal(key, full_shape, jnp.float32), -6.0, 6.0)
    return fresh.astype(jnp.bfloat16)


def touch_ends(entries, own_key, least, largest):
    extent = entries.shape
    index_at = [jax.random.randint(jax.random.fold_in(own_key, axis), (), 0, extent[axis]) for axis in range(len(extent))]
    entries = entries.at[tuple(index_at)].set(least)
    longest = extent.index(max(extent))
    index_at[longest] = (index_at[longest] + 1) % extent[longest]
    return entries.at[tuple(index_at)].set(largest)


def levels(own_key, dims, pieces, smallest, largest):
    def one(dim, shards_of):
        heights = jax.random.uniform(jax.random.fold_in(jax.random.fold_in(own_key, 6), dim), (shards_of,), jnp.float32, smallest / len(pieces), largest / len(pieces))
        return jnp.repeat(jnp.exp(heights), dims[dim] // shards_of).reshape((-1,) + (1,) * (len(dims) - dim - 1))

    level = one(*pieces[0])
    for cut in pieces[1:]:
        level = level * one(*cut)
    return level


def centred(stream_key, extent, scale, limit, cuts=(), kind=jnp.bfloat16):
    values = jax.random.normal(stream_key, extent, jnp.float32) * scale
    if len(cuts) > 0:
        values = levels(stream_key, extent, cuts, -0.22, 0.18) * values
    return jnp.clip(values, min=-limit, max=limit).astype(kind)


def setup_inputs(seed: int = 0) -> dict:
    seeds = jax.random.split(jax.random.key(seed), 6)
    query_vectors = draw_query_vectors(jax.random.fold_in(seeds[5], 71), 0)
    key_vectors = draw_key_vectors(jax.random.fold_in(seeds[5], 71), 0)
    value_vectors = centred(seeds[2], (VIEWS, FRAMES, ROWS, COLS, FEAT), 1.0, 6.0, ((0, 8), (1, 16), (2, 2)))
    out_grad = centred(seeds[3], (VIEWS, FRAMES, ROWS, COLS, FEAT), 1.0, 6.0, ((0, 8), (1, 16), (2, 2)))
    epi_rows = touch_ends(jax.random.randint(seeds[4], (VIEWS, FRAMES, N_HEIGHT, VIEWS - 1), 0, ROWS), jax.random.fold_in(seeds[4], 1), 0, ROWS - 1).astype(jnp.int32)
    return dict(query_vectors=query_vectors, key_vectors=key_vectors, value_vectors=value_vectors, out_grad=out_grad, epi_rows=epi_rows)


def head_pass(query_rows, key_rows, value_rows, grad_rows, usable, score_scale):
    query_wide = query_rows.astype(jnp.float32)
    key_wide = key_rows.astype(jnp.float32)
    value_wide = value_rows.astype(jnp.float32)
    grad_wide = grad_rows.astype(jnp.float32)
    scores = jnp.einsum('ne,me->nm', query_wide, key_wide) * score_scale
    scores = jnp.where(usable[None, :], scores, -1e30)
    row_max = jnp.max(scores, axis=1, keepdims=True)
    weights = jnp.exp(scores - row_max)
    normalized = weights / jnp.sum(weights, axis=1, keepdims=True)
    normalized_low = lax.optimization_barrier(normalized.astype(jnp.bfloat16)).astype(jnp.float32)
    attended = jnp.einsum('nm,me->ne', normalized_low, value_wide).astype(jnp.bfloat16)
    grad_weights = jnp.einsum('ne,me->nm', grad_wide, value_wide)
    row_delta = jnp.sum(grad_wide * attended.astype(jnp.float32), axis=1, keepdims=True)
    score_grad = lax.optimization_barrier((normalized * (grad_weights - row_delta)).astype(jnp.bfloat16)).astype(jnp.float32)
    query_grad = (jnp.einsum('nm,me->ne', score_grad, key_wide) * score_scale).astype(jnp.bfloat16)
    key_terms = jnp.einsum('nm,ne->me', score_grad, query_wide) * score_scale
    value_terms = jnp.einsum('nm,ne->me', normalized_low, grad_wide)
    return attended, query_grad, key_terms, value_terms


def reference(query_vectors, key_vectors, value_vectors, out_grad, epi_rows):
    view_count, frame_count, row_count, columns, features = query_vectors.shape
    head_count = features // HEAD_DIM
    band_count = row_count // TILE_ROWS
    tokens = TILE_ROWS * columns
    score_scale = HEAD_DIM ** -0.5
    epi_table = epi_rows.astype(jnp.int32)

    def tiled(array):
        return array.reshape(view_count, frame_count, band_count, tokens, head_count, HEAD_DIM)

    query_tiles = tiled(query_vectors)
    key_tiles = tiled(key_vectors)
    value_tiles = tiled(value_vectors)
    grad_tiles = tiled(out_grad)
    key_lines = key_vectors.reshape(view_count, frame_count, row_count, columns, head_count, HEAD_DIM)
    value_lines = value_vectors.reshape(view_count, frame_count, row_count, columns, head_count, HEAD_DIM)

    def one_tile(tile_index):
        view_at = tile_index // (frame_count * band_count)
        frame_at = (tile_index // band_count) % frame_count
        band_at = tile_index % band_count
        earlier = jnp.maximum(frame_at - 1, 0)
        key_parts = [key_tiles[view_at, frame_at, band_at], key_tiles[view_at, earlier, band_at]]
        value_parts = [value_tiles[view_at, frame_at, band_at], value_tiles[view_at, earlier, band_at]]
        for offset in range(1, view_count):
            source = (view_at + offset) % view_count
            row_at = epi_table[view_at, frame_at, band_at, offset - 1]
            key_parts.append(key_lines[source, frame_at, row_at])
            value_parts.append(value_lines[source, frame_at, row_at])
        key_set = jnp.concatenate(key_parts, axis=0)
        value_set = jnp.concatenate(value_parts, axis=0)
        usable = jnp.concatenate([jnp.ones((tokens,), bool), jnp.broadcast_to(frame_at > 0, (tokens,)), jnp.ones(((view_count - 1) * columns,), bool)])

        def one_head(parts):
            return head_pass(parts[0], parts[1], parts[2], parts[3], usable, score_scale)

        head_major = tuple(jnp.moveaxis(array, 1, 0) for array in (query_tiles[view_at, frame_at, band_at], key_set, value_set, grad_tiles[view_at, frame_at, band_at]))
        attended, query_grad, key_terms, value_terms = lax.map(one_head, head_major)
        attended = jnp.moveaxis(attended, 0, 1)
        query_grad = jnp.moveaxis(query_grad, 0, 1)
        key_terms = jnp.moveaxis(key_terms, 0, 1)
        value_terms = jnp.moveaxis(value_terms, 0, 1)
        far_shape = (view_count - 1, columns, head_count, HEAD_DIM)
        return (attended, query_grad, key_terms[:tokens], value_terms[:tokens],
                key_terms[tokens:2 * tokens].astype(jnp.bfloat16), value_terms[tokens:2 * tokens].astype(jnp.bfloat16),
                key_terms[2 * tokens:].astype(jnp.bfloat16).reshape(far_shape), value_terms[2 * tokens:].astype(jnp.bfloat16).reshape(far_shape))

    results = lax.map(one_tile, jnp.arange(view_count * frame_count * band_count, dtype=jnp.int32))
    sources = (jnp.arange(view_count, dtype=jnp.int32)[:, None, None, None] + jnp.arange(1, view_count, dtype=jnp.int32)[None, None, None, :]) % view_count
    sources = jnp.broadcast_to(sources, epi_table.shape).astype(jnp.int32)
    frames_at = jnp.broadcast_to(jnp.arange(frame_count, dtype=jnp.int32)[None, :, None, None], epi_table.shape).astype(jnp.int32)

    def assemble(own_terms, earlier_terms, far_terms):
        grid = own_terms.reshape(view_count, frame_count, band_count, tokens, head_count, HEAD_DIM)
        later = earlier_terms.reshape(view_count, frame_count, band_count, tokens, head_count, HEAD_DIM).astype(jnp.float32)
        grid = grid.at[:, :-1].add(later[:, 1:])
        grid = grid.reshape(view_count, frame_count, row_count, columns, head_count, HEAD_DIM)
        far_grid = far_terms.reshape(view_count, frame_count, band_count, view_count - 1, columns, head_count, HEAD_DIM).astype(jnp.float32)
        grid = grid.at[sources, frames_at, epi_table].add(far_grid)
        return grid.astype(jnp.bfloat16).reshape(query_vectors.shape)

    attended = results[0].reshape(query_vectors.shape)
    query_grad = results[1].reshape(query_vectors.shape)
    key_grad = assemble(results[2], results[4], results[6])
    value_grad = assemble(results[3], results[5], results[7])
    return (attended, query_grad, key_grad, value_grad)
```

```python
import functools

import jax
import jax.numpy as jnp
from jax import lax
from jax.experimental import pallas as pl
from jax.experimental.pallas import tpu as pltpu
from jax.sharding import PartitionSpec as P

HEAD_DIM = 128
MESH = pl.DeviceIdType.MESH
F32 = jnp.float32
BF16 = jnp.bfloat16


def dot(a, b, over_a, over_b):
    return lax.dot_general(a, b, (((over_a,), (over_b,)), ((), ())), preferred_element_type=F32)


def kernel(
    views, frames, columns, tile_rows, heads,
    q_in, k_in, v_in, g_in, epi, holds, o_out, dq_out, dk_out, dv_out,
    q_buf, g_buf, kv_buf, line_buf, pick, terms, own, later, back, results,
    local_sem, pre_send, pre_recv, frame_send, frame_recv, line_send, line_recv,
    later_send, later_recv, back_send, back_recv, post_send, post_recv, out_sem,
):
    view = lax.axis_index("view")
    frame = lax.axis_index("tm")
    height = lax.axis_index("height")
    other = 1 - height
    tokens = tile_rows * columns
    others = views - 1
    set_size = 2 * tokens + others * columns
    scale = HEAD_DIM ** (-0.5)
    inputs = (q_in, k_in, v_in, g_in)
    outputs = (o_out, dq_out, dk_out, dv_out)
    partner = {"height": other}

    def requester(d):
        return lax.rem(view - d + views, views)

    def source(d):
        return lax.rem(view + d, views)

    def cols(group, j):
        return pl.ds(pl.multiple_of((group * heads + j) * HEAD_DIM, HEAD_DIM), HEAD_DIM)

    def landing(a, j, band):
        if a == 0:
            return q_buf.at[j, band]
        if a == 3:
            return g_buf.at[j, band]
        return kv_buf.at[j, a - 1, band, pl.ds(0, tokens)]

    def local_copy(a, j):
        return pltpu.make_async_copy(
            inputs[a].at[:, cols(height, j)], landing(a, j, height), local_sem.at[j, a]
        )

    def pre_copy(a, j):
        return pltpu.make_async_remote_copy(
            src_ref=inputs[a].at[:, cols(other, j)],
            dst_ref=landing(a, j, height),
            send_sem=pre_send.at[j, a],
            recv_sem=pre_recv.at[j, a],
            device_id=partner,
            device_id_type=MESH,
        )

    def pre_arrival(a, j):
        return pltpu.make_async_remote_copy(
            src_ref=inputs[a].at[:, cols(other, j)],
            dst_ref=landing(a, j, other),
            send_sem=pre_send.at[j, a],
            recv_sem=pre_recv.at[j, a],
            device_id=partner,
            device_id_type=MESH,
        )

    def frame_copy(j):
        return pltpu.make_async_remote_copy(
            src_ref=kv_buf.at[j, :, :, pl.ds(0, tokens)],
            dst_ref=kv_buf.at[j, :, :, pl.ds(tokens, tokens)],
            send_sem=frame_send.at[j],
            recv_sem=frame_recv.at[j],
            device_id={"tm": lax.rem(frame + 1, frames)},
            device_id_type=MESH,
        )

    def later_copy(j):
        return pltpu.make_async_remote_copy(
            src_ref=terms.at[j, :, :, pl.ds(0, tokens)],
            dst_ref=later.at[j],
            send_sem=later_send.at[j],
            recv_sem=later_recv.at[j],
            device_id={"tm": lax.rem(frame + frames - 1, frames)},
            device_id_type=MESH,
        )

    def line_copy(d, j):
        at = (d - 1) * columns
        return pltpu.make_async_remote_copy(
            src_ref=line_buf.at[j, :, :, pl.ds(at, columns)],
            dst_ref=kv_buf.at[j, :, :, pl.ds(2 * tokens + at, columns)],
            send_sem=line_send.at[j, d - 1],
            recv_sem=line_recv.at[j, d - 1],
            device_id={"view": requester(d)},
            device_id_type=MESH,
        )

    def back_copy(d, j):
        at = (d - 1) * columns
        return pltpu.make_async_remote_copy(
            src_ref=terms.at[j, :, :, pl.ds(tokens + at, columns)],
            dst_ref=back.at[j, :, :, pl.ds(at, columns)],
            send_sem=back_send.at[j, d - 1],
            recv_sem=back_recv.at[j, d - 1],
            device_id={"view": source(d)},
            device_id_type=MESH,
        )

    def out_copy(a, j):
        return pltpu.make_async_copy(
            results.at[a, j, height], outputs[a].at[:, cols(height, j)], out_sem.at[j, a]
        )

    def post_copy(a, j):
        return pltpu.make_async_remote_copy(
            src_ref=results.at[a, j, other],
            dst_ref=outputs[a].at[:, cols(height, j)],
            send_sem=post_send.at[j, a],
            recv_sem=post_recv.at[j, a],
            device_id=partner,
            device_id_type=MESH,
        )

    def post_arrival(a, j):
        return pltpu.make_async_remote_copy(
            src_ref=results.at[a, j, other],
            dst_ref=outputs[a].at[:, cols(other, j)],
            send_sem=post_send.at[j, a],
            recv_sem=post_recv.at[j, a],
            device_id=partner,
            device_id_type=MESH,
        )

    def start_local(j, carry):
        for a in range(4):
            local_copy(a, j).start()
        return carry

    lax.fori_loop(0, heads, start_local, 0)

    barrier = pltpu.get_barrier_semaphore()

    def greet(device):
        pl.semaphore_signal(barrier, inc=1, device_id=device, device_id_type=MESH)

    greet(partner)
    for d in range(1, views):
        greet({"view": source(d)})
    greet({"tm": lax.rem(frame + 1, frames)})
    greet({"tm": lax.rem(frame + frames - 1, frames)})
    pl.semaphore_wait(barrier, views + 2)

    def start_pre(j):
        for a in (1, 2, 0, 3):
            pre_copy(a, j).start()

    start_pre(0)
    start_pre(1)

    @pl.when(frame == 0)
    def _():
        kv_buf[:, :, :, tokens : 2 * tokens, :] = jnp.zeros(
            (heads, 2, 2, tokens, HEAD_DIM), BF16
        )

    @pl.when(frame == frames - 1)
    def _():
        later[...] = jnp.zeros(later.shape, BF16)

    def gather(j):
        for a in range(4):
            local_copy(a, j).wait()
            pre_arrival(a, j).wait_recv()

        @pl.when(frame < frames - 1)
        def _():
            frame_copy(j).start()

        for side in range(2):
            for band in range(2):
                for row in range(tile_rows):
                    pick[side, band * tile_rows + row] = kv_buf[
                        j, side, band, row * columns : (row + 1) * columns, :
                    ]
        for d in range(1, views):
            for band in range(2):
                row = epi[requester(d), 0, band, d - 1]
                for side in range(2):
                    line_buf[j, side, band, (d - 1) * columns : d * columns, :] = pick[side, row]
            line_copy(d, j).start()

        @pl.when(j < heads - 2)
        def _():
            for a in range(4):
                pre_copy(a, j).wait_send()
            start_pre(j + 2)

    first_row = lax.broadcasted_iota(jnp.int32, (set_size, 1), 0)
    masked = (first_row >= tokens) & (first_row < 2 * tokens) & (frame == 0)
    bias = jnp.where(masked, -1e30, 0.0).astype(F32)

    def attend(j, band):
        queries = q_buf[j, band]
        grads = g_buf[j, band]
        keys = kv_buf[j, 0, band]
        values = kv_buf[j, 1, band]
        scores = dot(keys, queries, 1, 1) * scale + bias
        weights = jnp.exp(scores - jnp.max(scores, axis=0, keepdims=True))
        probs = weights * (1.0 / jnp.sum(weights, axis=0, keepdims=True))
        probs_low = probs.astype(BF16)
        attended = dot(values, probs_low, 0, 0).astype(BF16)
        results[0, j, band] = attended.astype(F32).T.astype(BF16)
        delta = jnp.sum(
            grads.astype(F32).T * attended.astype(F32), axis=0, keepdims=True
        )
        dprobs = dot(values, grads, 1, 1)
        dscores = (probs * (dprobs - delta)).astype(BF16)
        dq = dot(keys, dscores, 0, 0) * scale
        results[1, j, band] = dq.T.astype(BF16)
        dk = dot(dscores, queries, 1, 0) * scale
        dv = dot(probs_low, grads, 1, 0)
        for side, term in ((0, dk), (1, dv)):
            own[j, side, band] = term[:tokens]
            terms[j, side, band] = term[tokens:].astype(BF16)

    def compute(j):
        @pl.when(frame > 0)
        def _():
            frame_copy(j).wait_recv()

        for d in range(1, views):
            line_copy(d, j).wait_recv()

        def one_band(band, carry):
            attend(j, band)
            return carry

        lax.fori_loop(0, 2, one_band, 0)

        @pl.when(frame > 0)
        def _():
            later_copy(j).start()

        for d in range(1, views):
            back_copy(d, j).start()
        for a in range(2):
            post_copy(a, j).start()
            out_copy(a, j).start()

    def settle(j):
        @pl.when(frame < frames - 1)
        def _():
            later_copy(j).wait_recv()

        for d in range(1, views):
            back_copy(d, j).wait_recv()

        step = 16
        chunks = columns // step

        def chunk(i, carry):
            side = i // chunks
            at = pl.multiple_of((i % chunks) * step, step)
            sums = []
            for row in range(2 * tile_rows):
                here = pl.ds((row % tile_rows) * columns + at, step)
                band = row // tile_rows
                sums.append(own[j, side, band, here, :] + later[j, side, band, here, :].astype(F32))
            for d in range(1, views):
                for band in range(2):
                    slot = back[j, side, band, pl.ds((d - 1) * columns + at, step), :].astype(F32)
                    for row in range(2 * tile_rows):
                        sums[row] += slot * holds[band, d - 1, row]
            for row in range(2 * tile_rows):
                here = pl.ds((row % tile_rows) * columns + at, step)
                results[2 + side, j, row // tile_rows, here, :] = sums[row].astype(BF16)
            return carry

        lax.fori_loop(0, 2 * chunks, chunk, 0)
        for a in range(2, 4):
            post_copy(a, j).start()
            out_copy(a, j).start()

    def stage(t, carry):
        @pl.when(t < heads)
        def _():
            gather(t)

        @pl.when((t >= 1) & (t < heads + 1))
        def _():
            compute(t - 1)

        @pl.when(t >= 2)
        def _():
            settle(t - 2)

        return carry

    lax.fori_loop(0, heads + 2, stage, 0)

    def drain(j, carry):
        @pl.when(j >= heads - 2)
        def _():
            for a in range(4):
                pre_copy(a, j).wait_send()

        @pl.when(frame < frames - 1)
        def _():
            frame_copy(j).wait_send()

        @pl.when(frame > 0)
        def _():
            later_copy(j).wait_send()

        for d in range(1, views):
            line_copy(d, j).wait_send()
            back_copy(d, j).wait_send()
        for a in range(4):
            post_copy(a, j).wait_send()
            post_arrival(a, j).wait_recv()
            out_copy(a, j).wait()
        return carry

    lax.fori_loop(0, heads, drain, 0)


def body(query_vectors, key_vectors, value_vectors, out_grad, epi_rows):
    views = lax.axis_size("view")
    frames = lax.axis_size("tm")
    bands = lax.axis_size("height")
    shape = query_vectors.shape
    tile_rows, columns, features = shape[2:]
    tokens = tile_rows * columns
    heads = features // HEAD_DIM // bands
    others = views - 1
    set_size = 2 * tokens + others * columns
    flat = [x.reshape(tokens, features) for x in (query_vectors, key_vectors, value_vectors, out_grad)]
    viewers = jnp.arange(views, dtype=jnp.int32)
    theirs = (lax.axis_index("view") - viewers) % views
    asked = theirs[:, None] == jnp.arange(1, views, dtype=jnp.int32)[None, :]
    rows = jnp.sum(epi_rows[:, 0] * asked[:, None, :], axis=0)
    holds = (rows[:, :, None] == jnp.arange(bands * tile_rows, dtype=jnp.int32)).astype(F32)
    dma = pltpu.SemaphoreType.DMA
    outs = pl.pallas_call(
        functools.partial(kernel, views, frames, columns, tile_rows, heads),
        out_shape=[jax.ShapeDtypeStruct((tokens, features), BF16)] * 4,
        in_specs=[pl.BlockSpec(memory_space=pl.ANY)] * 4 + [pl.BlockSpec(memory_space=pltpu.SMEM)] * 2,
        out_specs=[pl.BlockSpec(memory_space=pl.ANY)] * 4,
        scratch_shapes=[
            pltpu.VMEM((heads, 2, tokens, HEAD_DIM), BF16),
            pltpu.VMEM((heads, 2, tokens, HEAD_DIM), BF16),
            pltpu.VMEM((heads, 2, 2, set_size, HEAD_DIM), BF16),
            pltpu.VMEM((heads, 2, 2, others * columns, HEAD_DIM), BF16),
            pltpu.VMEM((2, 2 * tile_rows, columns, HEAD_DIM), BF16),
            pltpu.VMEM((heads, 2, 2, set_size - tokens, HEAD_DIM), BF16),
            pltpu.VMEM((heads, 2, 2, tokens, HEAD_DIM), F32),
            pltpu.VMEM((heads, 2, 2, tokens, HEAD_DIM), BF16),
            pltpu.VMEM((heads, 2, 2, others * columns, HEAD_DIM), BF16),
            pltpu.VMEM((4, heads, 2, tokens, HEAD_DIM), BF16),
            dma((heads, 4)),
            dma((heads, 4)),
            dma((heads, 4)),
            dma((heads,)),
            dma((heads,)),
            dma((heads, others)),
            dma((heads, others)),
            dma((heads,)),
            dma((heads,)),
            dma((heads, others)),
            dma((heads, others)),
            dma((heads, 4)),
            dma((heads, 4)),
            dma((heads, 4)),
        ],
        compiler_params=pltpu.CompilerParams(
            collective_id=0, has_side_effects=True, vmem_limit_bytes=52 * 1024 * 1024
        ),
        name="attention",
    )(*flat, epi_rows, holds)
    return tuple(x.reshape(shape) for x in outs)


def solution(mesh):
    tiled = P("view", "tm", "height", None, None)
    return jax.shard_map(
        body,
        mesh=mesh,
        in_specs=(tiled, tiled, tiled, tiled, P(None, "tm", None, None)),
        out_specs=(tiled, tiled, tiled, tiled),
        check_vma=False,
    )
```

```python
import functools

import jax
import jax.numpy as jnp
from jax import lax
from jax.experimental import pallas as pl
from jax.experimental.pallas import tpu as pltpu
from jax.sharding import PartitionSpec as P

HEAD_DIM = 128
RUN = 4
EARLY = 3
LAG_AHEAD = 0
LAG_COMPUTE = 2
LAG_BEHIND = 2
LAG_SETTLE = 3
MESH = pl.DeviceIdType.MESH
F32 = jnp.float32
BF16 = jnp.bfloat16


def dot(a, b, over_a, over_b):
    return lax.dot_general(a, b, (((over_a,), (over_b,)), ((), ())), preferred_element_type=F32)


def kernel(
    views, frames, columns, tile_rows, heads,
    q_in, k_in, v_in, g_in, epi, holds, o_out, dq_out, dk_out, dv_out,
    q_buf, g_buf, kv_buf, line_buf, pick, terms, own, later, back, results, ahead, behind,
    local_sem, pre_send, pre_recv, frame_send, frame_recv, line_send, line_recv,
    later_send, later_recv, ahead_send, ahead_recv, behind_send, behind_recv, back_send, back_recv, post_send, post_recv, out_sem,
):
    view = lax.axis_index("view")
    frame = lax.axis_index("tm")
    height = lax.axis_index("height")
    other = 1 - height
    tokens = tile_rows * columns
    others = views - 1
    set_size = 2 * tokens + others * columns
    scale = HEAD_DIM ** (-0.5)
    inputs = (q_in, k_in, v_in, g_in)
    outputs = (o_out, dq_out, dk_out, dv_out)
    partner = {"height": other}

    def requester(d):
        return lax.rem(view - d + views, views)

    def source(d):
        return lax.rem(view + d, views)

    def cols(group, j):
        return pl.ds(pl.multiple_of((group * heads + j) * HEAD_DIM, HEAD_DIM), HEAD_DIM)

    def landing(a, j, band):
        if a == 0:
            return q_buf.at[j, band]
        if a == 3:
            return g_buf.at[j, band]
        return kv_buf.at[j, a - 1, band, pl.ds(0, tokens)]

    def local_copy(a, j):
        return pltpu.make_async_copy(
            inputs[a].at[:, cols(height, j)], landing(a, j, height), local_sem.at[j, a]
        )

    def pre_copy(a, j):
        return pltpu.make_async_remote_copy(
            src_ref=inputs[a].at[:, cols(other, j)],
            dst_ref=landing(a, j, height),
            send_sem=pre_send.at[j, a],
            recv_sem=pre_recv.at[j, a],
            device_id=partner,
            device_id_type=MESH,
        )

    def pre_arrival(a, j):
        return pltpu.make_async_remote_copy(
            src_ref=inputs[a].at[:, cols(other, j)],
            dst_ref=landing(a, j, other),
            send_sem=pre_send.at[j, a],
            recv_sem=pre_recv.at[j, a],
            device_id=partner,
            device_id_type=MESH,
        )

    run_at = lax.rem(frame, RUN)
    run_start = frame - run_at

    def at_frame(f):
        return {"tm": lax.rem(f + frames, frames)}

    def remote(src, dst, send_sem, recv_sem, device):
        return pltpu.make_async_remote_copy(
            src_ref=src,
            dst_ref=dst,
            send_sem=send_sem,
            recv_sem=recv_sem,
            device_id=device,
            device_id_type=MESH,
        )

    def earlier_slot(p, j):
        return kv_buf.at[j, p // 2, p % 2, pl.ds(tokens, tokens)]

    def frame_copy(p, j):
        return remote(
            kv_buf.at[j, p // 2, p % 2, pl.ds(0, tokens)],
            earlier_slot(p, j),
            frame_send.at[j, p],
            frame_recv.at[j, p],
            at_frame(frame + 1),
        )

    def ahead_copy(p, j):
        return remote(
            kv_buf.at[j, p // 2, p % 2, pl.ds(0, tokens)],
            ahead.at[j],
            frame_send.at[j, p],
            ahead_recv.at[j],
            at_frame(run_start + p),
        )

    def ahead_pass(j):
        return remote(
            ahead.at[j],
            earlier_slot(run_at, j),
            ahead_send.at[j],
            frame_recv.at[j, run_at],
            at_frame(run_start + RUN),
        )

    def later_copy(p, j):
        return remote(
            terms.at[j, p // 2, p % 2, pl.ds(0, tokens)],
            later.at[j, p // 2, p % 2],
            later_send.at[j, p],
            later_recv.at[j, p],
            at_frame(frame - 1),
        )

    def behind_copy(p, j):
        return remote(
            terms.at[j, p // 2, p % 2, pl.ds(0, tokens)],
            behind.at[j],
            later_send.at[j, p],
            behind_recv.at[j],
            at_frame(run_start + p),
        )

    def behind_pass(j):
        return remote(
            behind.at[j],
            later.at[j, run_at // 2, run_at % 2],
            behind_send.at[j],
            later_recv.at[j, run_at],
            at_frame(run_start - 1),
        )

    passes_ahead = (run_at < RUN - 1) & (frame < frames - RUN)
    passes_behind = (run_at > 0) & (frame >= RUN)

    def send_frame(j):
        @pl.when(run_at < RUN - 1)
        def _():
            for p in range(RUN):
                frame_copy(p, j).start()

        @pl.when((run_at == RUN - 1) & (frame < frames - 1))
        def _():
            frame_copy(RUN - 1, j).start()
            for p in range(RUN - 1):
                ahead_copy(p, j).start()

    def send_later(j):
        @pl.when(run_at > 0)
        def _():
            for p in range(RUN):
                later_copy(p, j).start()

        @pl.when((run_at == 0) & (frame > 0))
        def _():
            later_copy(0, j).start()
            for p in range(1, RUN):
                behind_copy(p, j).start()

    def pass_ahead(j):
        @pl.when(passes_ahead)
        def _():
            remote(
                ahead.at[j], ahead.at[j], ahead_send.at[j], ahead_recv.at[j], at_frame(run_start + RUN)
            ).wait_recv()
            ahead_pass(j).start()

    def pass_behind(j):
        @pl.when(passes_behind)
        def _():
            remote(
                behind.at[j], behind.at[j], behind_send.at[j], behind_recv.at[j], at_frame(run_start - 1)
            ).wait_recv()
            behind_pass(j).start()

    def line_copy(d, j):
        at = (d - 1) * columns
        return pltpu.make_async_remote_copy(
            src_ref=line_buf.at[j, :, :, pl.ds(at, columns)],
            dst_ref=kv_buf.at[j, :, :, pl.ds(2 * tokens + at, columns)],
            send_sem=line_send.at[j, d - 1],
            recv_sem=line_recv.at[j, d - 1],
            device_id={"view": requester(d)},
            device_id_type=MESH,
        )

    def back_copy(d, j):
        at = (d - 1) * columns
        return pltpu.make_async_remote_copy(
            src_ref=terms.at[j, :, :, pl.ds(tokens + at, columns)],
            dst_ref=back.at[j, :, :, pl.ds(at, columns)],
            send_sem=back_send.at[j, d - 1],
            recv_sem=back_recv.at[j, d - 1],
            device_id={"view": source(d)},
            device_id_type=MESH,
        )

    def out_copy(a, j):
        return pltpu.make_async_copy(
            results.at[a, j, height], outputs[a].at[:, cols(height, j)], out_sem.at[j, a]
        )

    def post_copy(a, j):
        return pltpu.make_async_remote_copy(
            src_ref=results.at[a, j, other],
            dst_ref=outputs[a].at[:, cols(height, j)],
            send_sem=post_send.at[j, a],
            recv_sem=post_recv.at[j, a],
            device_id=partner,
            device_id_type=MESH,
        )

    def post_arrival(a, j):
        return pltpu.make_async_remote_copy(
            src_ref=results.at[a, j, other],
            dst_ref=outputs[a].at[:, cols(other, j)],
            send_sem=post_send.at[j, a],
            recv_sem=post_recv.at[j, a],
            device_id=partner,
            device_id_type=MESH,
        )

    def start_local(j, carry):
        for a in range(4):
            local_copy(a, j).start()
        return carry

    lax.fori_loop(0, heads, start_local, 0)

    barrier = pltpu.get_barrier_semaphore()

    def greet(device):
        pl.semaphore_signal(barrier, inc=1, device_id=device, device_id_type=MESH)

    greet(partner)
    for d in range(1, views):
        greet({"view": source(d)})
    for by in range(1, RUN + 1):
        greet(at_frame(frame + by))
        greet(at_frame(frame - by))
    pl.semaphore_wait(barrier, views + 2 * RUN)

    def start_pre(j):
        for a in (1, 2, 0, 3):
            pre_copy(a, j).start()

    for j in range(min(EARLY, heads)):
        start_pre(j)

    @pl.when(frame == 0)
    def _():
        kv_buf[:, :, :, tokens : 2 * tokens, :] = jnp.zeros(
            (heads, 2, 2, tokens, HEAD_DIM), BF16
        )

    @pl.when(frame == frames - 1)
    def _():
        later[...] = jnp.zeros(later.shape, BF16)

    def gather(j):
        for a in range(4):
            local_copy(a, j).wait()
            pre_arrival(a, j).wait_recv()

        send_frame(j)

        for side in range(2):
            for band in range(2):
                for row in range(tile_rows):
                    pick[side, band * tile_rows + row] = kv_buf[
                        j, side, band, row * columns : (row + 1) * columns, :
                    ]
        for d in range(1, views):
            for band in range(2):
                row = epi[requester(d), 0, band, d - 1]
                for side in range(2):
                    line_buf[j, side, band, (d - 1) * columns : d * columns, :] = pick[side, row]
            line_copy(d, j).start()

        @pl.when(j < heads - EARLY)
        def _():
            for a in range(4):
                pre_copy(a, j).wait_send()
            start_pre(j + EARLY)

    first_row = lax.broadcasted_iota(jnp.int32, (set_size, 1), 0)
    masked = (first_row >= tokens) & (first_row < 2 * tokens) & (frame == 0)
    bias = jnp.where(masked, -1e30, 0.0).astype(F32)

    def attend(j, band):
        queries = q_buf[j, band]
        grads = g_buf[j, band]
        keys = kv_buf[j, 0, band]
        values = kv_buf[j, 1, band]
        scores = dot(keys, queries, 1, 1) * scale + bias
        weights = jnp.exp(scores - jnp.max(scores, axis=0, keepdims=True))
        probs = weights * (1.0 / jnp.sum(weights, axis=0, keepdims=True))
        probs_low = probs.astype(BF16)
        attended = dot(values, probs_low, 0, 0).astype(BF16)
        results[0, j, band] = attended.astype(F32).T.astype(BF16)
        delta = jnp.sum(
            grads.astype(F32).T * attended.astype(F32), axis=0, keepdims=True
        )
        dprobs = dot(values, grads, 1, 1)
        dscores = (probs * (dprobs - delta)).astype(BF16)
        dq = dot(keys, dscores, 0, 0) * scale
        results[1, j, band] = dq.T.astype(BF16)
        dk = dot(dscores, queries, 1, 0) * scale
        dv = dot(probs_low, grads, 1, 0)
        for side, term in ((0, dk), (1, dv)):
            own[j, side, band] = term[:tokens]
            terms[j, side, band] = term[tokens:].astype(BF16)

    def compute(j):
        @pl.when(frame > 0)
        def _():
            for p in range(RUN):
                frame_copy(p, j).wait_recv()

        for d in range(1, views):
            line_copy(d, j).wait_recv()

        def one_band(band, carry):
            attend(j, band)
            return carry

        lax.fori_loop(0, 2, one_band, 0)

        send_later(j)

        for d in range(1, views):
            back_copy(d, j).start()
        for a in range(2):
            post_copy(a, j).start()
            out_copy(a, j).start()

    def settle(j):
        @pl.when(frame < frames - 1)
        def _():
            for p in range(RUN):
                later_copy(p, j).wait_recv()

        for d in range(1, views):
            back_copy(d, j).wait_recv()

        step = 16
        chunks = columns // step

        def chunk(i, carry):
            side = i // chunks
            at = pl.multiple_of((i % chunks) * step, step)
            sums = []
            for row in range(2 * tile_rows):
                here = pl.ds((row % tile_rows) * columns + at, step)
                band = row // tile_rows
                sums.append(own[j, side, band, here, :] + later[j, side, band, here, :].astype(F32))
            for d in range(1, views):
                for band in range(2):
                    slot = back[j, side, band, pl.ds((d - 1) * columns + at, step), :].astype(F32)
                    for row in range(2 * tile_rows):
                        sums[row] += slot * holds[band, d - 1, row]
            for row in range(2 * tile_rows):
                here = pl.ds((row % tile_rows) * columns + at, step)
                results[2 + side, j, row // tile_rows, here, :] = sums[row].astype(BF16)
            return carry

        lax.fori_loop(0, 2 * chunks, chunk, 0)
        for a in range(2, 4):
            post_copy(a, j).start()
            out_copy(a, j).start()

    def stage(t, carry):
        def at_stage(lag, step):
            @pl.when((t >= lag) & (t < heads + lag))
            def _():
                step(t - lag)

        at_stage(0, gather)
        at_stage(LAG_COMPUTE, compute)
        at_stage(LAG_AHEAD, pass_ahead)
        at_stage(LAG_SETTLE, settle)
        at_stage(LAG_BEHIND, pass_behind)
        return carry

    lax.fori_loop(0, heads + LAG_SETTLE, stage, 0)

    def drain(j, carry):
        @pl.when(j >= heads - EARLY)
        def _():
            for a in range(4):
                pre_copy(a, j).wait_send()

        @pl.when(frame < frames - 1)
        def _():
            for p in range(RUN):
                frame_copy(p, j).wait_send()

        @pl.when(frame > 0)
        def _():
            for p in range(RUN):
                later_copy(p, j).wait_send()

        @pl.when(passes_ahead)
        def _():
            ahead_pass(j).wait_send()

        @pl.when(passes_behind)
        def _():
            behind_pass(j).wait_send()

        for d in range(1, views):
            line_copy(d, j).wait_send()
            back_copy(d, j).wait_send()
        for a in range(4):
            post_copy(a, j).wait_send()
            post_arrival(a, j).wait_recv()
            out_copy(a, j).wait()
        return carry

    lax.fori_loop(0, heads, drain, 0)


def body(query_vectors, key_vectors, value_vectors, out_grad, epi_rows):
    views = lax.axis_size("view")
    frames = lax.axis_size("tm")
    bands = lax.axis_size("height")
    shape = query_vectors.shape
    tile_rows, columns, features = shape[2:]
    tokens = tile_rows * columns
    heads = features // HEAD_DIM // bands
    others = views - 1
    set_size = 2 * tokens + others * columns
    flat = [x.reshape(tokens, features) for x in (query_vectors, key_vectors, value_vectors, out_grad)]
    viewers = jnp.arange(views, dtype=jnp.int32)
    theirs = (lax.axis_index("view") - viewers) % views
    asked = theirs[:, None] == jnp.arange(1, views, dtype=jnp.int32)[None, :]
    rows = jnp.sum(epi_rows[:, 0] * asked[:, None, :], axis=0)
    holds = (rows[:, :, None] == jnp.arange(bands * tile_rows, dtype=jnp.int32)).astype(F32)
    dma = pltpu.SemaphoreType.DMA
    outs = pl.pallas_call(
        functools.partial(kernel, views, frames, columns, tile_rows, heads),
        out_shape=[jax.ShapeDtypeStruct((tokens, features), BF16)] * 4,
        in_specs=[pl.BlockSpec(memory_space=pl.ANY)] * 4 + [pl.BlockSpec(memory_space=pltpu.SMEM)] * 2,
        out_specs=[pl.BlockSpec(memory_space=pl.ANY)] * 4,
        scratch_shapes=[
            pltpu.VMEM((heads, 2, tokens, HEAD_DIM), BF16),
            pltpu.VMEM((heads, 2, tokens, HEAD_DIM), BF16),
            pltpu.VMEM((heads, 2, 2, set_size, HEAD_DIM), BF16),
            pltpu.VMEM((heads, 2, 2, others * columns, HEAD_DIM), BF16),
            pltpu.VMEM((2, 2 * tile_rows, columns, HEAD_DIM), BF16),
            pltpu.VMEM((heads, 2, 2, set_size - tokens, HEAD_DIM), BF16),
            pltpu.VMEM((heads, 2, 2, tokens, HEAD_DIM), F32),
            pltpu.VMEM((heads, 2, 2, tokens, HEAD_DIM), BF16),
            pltpu.VMEM((heads, 2, 2, others * columns, HEAD_DIM), BF16),
            pltpu.VMEM((4, heads, 2, tokens, HEAD_DIM), BF16),
            pltpu.VMEM((heads, tokens, HEAD_DIM), BF16),
            pltpu.VMEM((heads, tokens, HEAD_DIM), BF16),
            dma((heads, 4)),
            dma((heads, 4)),
            dma((heads, 4)),
            dma((heads, RUN)),
            dma((heads, RUN)),
            dma((heads, others)),
            dma((heads, others)),
            dma((heads, RUN)),
            dma((heads, RUN)),
            dma((heads,)),
            dma((heads,)),
            dma((heads,)),
            dma((heads,)),
            dma((heads, others)),
            dma((heads, others)),
            dma((heads, 4)),
            dma((heads, 4)),
            dma((heads, 4)),
        ],
        compiler_params=pltpu.CompilerParams(
            collective_id=0, has_side_effects=True, vmem_limit_bytes=52 * 1024 * 1024
        ),
        name="attention",
    )(*flat, epi_rows, holds)
    return tuple(x.reshape(shape) for x in outs)


def solution(mesh):
    tiled = P("view", "tm", "height", None, None)
    return jax.shard_map(
        body,
        mesh=mesh,
        in_specs=(tiled, tiled, tiled, tiled, P(None, "tm", None, None)),
        out_specs=(tiled, tiled, tiled, tiled),
        check_vma=False,
    )
```

```python
import functools

import jax
import jax.numpy as jnp
from jax import lax
from jax.experimental import pallas as pl
from jax.experimental.pallas import tpu as pltpu
from jax.sharding import PartitionSpec as P

HEAD_DIM = 128
RUN = 4
RELAYED = 5
EARLY = 3
QUERIES_BEHIND = 2
LAG_AHEAD = 0
LAG_COMPUTE = 3
LAG_BEHIND = 3
LAG_SETTLE = 4
MESH = pl.DeviceIdType.MESH
F32 = jnp.float32
BF16 = jnp.bfloat16


def dot(a, b, over_a, over_b):
    return lax.dot_general(a, b, (((over_a,), (over_b,)), ((), ())), preferred_element_type=F32)


def kernel(
    views, frames, columns, tile_rows, heads,
    q_in, k_in, v_in, g_in, epi, holds, o_out, dq_out, dk_out, dv_out,
    q_buf, g_buf, kv_buf, line_buf, pick, terms, own, later, back, results, ahead, behind,
    local_sem, pre_send, pre_recv, frame_send, frame_recv, line_send, line_recv,
    later_send, later_recv, ahead_send, ahead_recv, behind_send, behind_recv, back_send, back_recv, post_send, post_recv, out_sem,
):
    view = lax.axis_index("view")
    frame = lax.axis_index("tm")
    height = lax.axis_index("height")
    other = 1 - height
    tokens = tile_rows * columns
    others = views - 1
    set_size = 2 * tokens + others * columns
    scale = HEAD_DIM ** (-0.5)
    inputs = (q_in, k_in, v_in, g_in)
    outputs = (o_out, dq_out, dk_out, dv_out)
    partner = {"height": other}

    def requester(d):
        return lax.rem(view - d + views, views)

    def source(d):
        return lax.rem(view + d, views)

    def cols(group, j):
        return pl.ds(pl.multiple_of((group * heads + j) * HEAD_DIM, HEAD_DIM), HEAD_DIM)

    def landing(a, j, band):
        if a == 0:
            return q_buf.at[j, band]
        if a == 3:
            return g_buf.at[j, band]
        return kv_buf.at[j, a - 1, band, pl.ds(0, tokens)]

    def local_copy(a, j):
        return pltpu.make_async_copy(
            inputs[a].at[:, cols(height, j)], landing(a, j, height), local_sem.at[j, a]
        )

    def pre_copy(a, j):
        return pltpu.make_async_remote_copy(
            src_ref=inputs[a].at[:, cols(other, j)],
            dst_ref=landing(a, j, height),
            send_sem=pre_send.at[j, a],
            recv_sem=pre_recv.at[j, a],
            device_id=partner,
            device_id_type=MESH,
        )

    def pre_arrival(a, j):
        return pltpu.make_async_remote_copy(
            src_ref=inputs[a].at[:, cols(other, j)],
            dst_ref=landing(a, j, other),
            send_sem=pre_send.at[j, a],
            recv_sem=pre_recv.at[j, a],
            device_id=partner,
            device_id_type=MESH,
        )

    run_at = lax.rem(frame, RUN)
    run_start = frame - run_at

    def at_frame(f):
        return {"tm": lax.rem(f + frames, frames)}

    def remote(src, dst, send_sem, recv_sem, device):
        return pltpu.make_async_remote_copy(
            src_ref=src,
            dst_ref=dst,
            send_sem=send_sem,
            recv_sem=recv_sem,
            device_id=device,
            device_id_type=MESH,
        )

    def earlier_slot(p, j):
        return kv_buf.at[j, p // 2, p % 2, pl.ds(tokens, tokens)]

    def frame_copy(p, j):
        return remote(
            kv_buf.at[j, p // 2, p % 2, pl.ds(0, tokens)],
            earlier_slot(p, j),
            frame_send.at[j, p],
            frame_recv.at[j, p],
            at_frame(frame + 1),
        )

    def ahead_copy(p, j):
        return remote(
            kv_buf.at[j, p // 2, p % 2, pl.ds(0, tokens)],
            ahead.at[j],
            frame_send.at[j, p],
            ahead_recv.at[j],
            at_frame(run_start + p),
        )

    def ahead_pass(j):
        return remote(
            ahead.at[j],
            earlier_slot(run_at, j),
            ahead_send.at[j],
            frame_recv.at[j, run_at],
            at_frame(run_start + RUN),
        )

    def later_copy(p, j):
        return remote(
            terms.at[j, p // 2, p % 2, pl.ds(0, tokens)],
            later.at[j, p // 2, p % 2],
            later_send.at[j, p],
            later_recv.at[j, p],
            at_frame(frame - 1),
        )

    def behind_copy(p, j):
        return remote(
            terms.at[j, p // 2, p % 2, pl.ds(0, tokens)],
            behind.at[j],
            later_send.at[j, p],
            behind_recv.at[j],
            at_frame(run_start + p),
        )

    def behind_pass(j):
        return remote(
            behind.at[j],
            later.at[j, run_at // 2, run_at % 2],
            behind_send.at[j],
            later_recv.at[j, run_at],
            at_frame(run_start - 1),
        )

    passes_ahead = (run_at < RUN - 1) & (frame < frames - RUN)
    passes_behind = (run_at > 0) & (frame >= RUN)

    def send_frame(j):
        @pl.when(run_at < RUN - 1)
        def _():
            for p in range(RUN):
                frame_copy(p, j).start()

        @pl.when((run_at == RUN - 1) & (frame < frames - 1))
        def _():
            frame_copy(RUN - 1, j).start()
            for p in range(RUN - 1):
                ahead_copy(p, j).start()

    def send_later(j):
        @pl.when(run_at > 0)
        def _():
            for p in range(RUN):
                later_copy(p, j).start()

        @pl.when((run_at == 0) & (frame > 0) & (j < RELAYED))
        def _():
            later_copy(0, j).start()
            for p in range(1, RUN):
                behind_copy(p, j).start()

        @pl.when((run_at == 0) & (frame > 0) & (j >= RELAYED))
        def _():
            for p in range(RUN):
                later_copy(p, j).start()

    def pass_ahead(j):
        @pl.when(passes_ahead)
        def _():
            remote(
                ahead.at[j], ahead.at[j], ahead_send.at[j], ahead_recv.at[j], at_frame(run_start + RUN)
            ).wait_recv()
            ahead_pass(j).start()

    def pass_behind(j):
        @pl.when(passes_behind & (j < RELAYED))
        def _():
            remote(
                behind.at[j], behind.at[j], behind_send.at[j], behind_recv.at[j], at_frame(run_start - 1)
            ).wait_recv()
            behind_pass(j).start()

    def line_copy(d, j):
        at = (d - 1) * columns
        return pltpu.make_async_remote_copy(
            src_ref=line_buf.at[j, :, :, pl.ds(at, columns)],
            dst_ref=kv_buf.at[j, :, :, pl.ds(2 * tokens + at, columns)],
            send_sem=line_send.at[j, d - 1],
            recv_sem=line_recv.at[j, d - 1],
            device_id={"view": requester(d)},
            device_id_type=MESH,
        )

    def back_copy(d, j):
        at = (d - 1) * columns
        return pltpu.make_async_remote_copy(
            src_ref=terms.at[j, :, :, pl.ds(tokens + at, columns)],
            dst_ref=back.at[j, :, :, pl.ds(at, columns)],
            send_sem=back_send.at[j, d - 1],
            recv_sem=back_recv.at[j, d - 1],
            device_id={"view": source(d)},
            device_id_type=MESH,
        )

    def out_copy(a, j):
        return pltpu.make_async_copy(
            results.at[a, j, height], outputs[a].at[:, cols(height, j)], out_sem.at[j, a]
        )

    def post_copy(a, j):
        return pltpu.make_async_remote_copy(
            src_ref=results.at[a, j, other],
            dst_ref=outputs[a].at[:, cols(height, j)],
            send_sem=post_send.at[j, a],
            recv_sem=post_recv.at[j, a],
            device_id=partner,
            device_id_type=MESH,
        )

    def post_arrival(a, j):
        return pltpu.make_async_remote_copy(
            src_ref=results.at[a, j, other],
            dst_ref=outputs[a].at[:, cols(other, j)],
            send_sem=post_send.at[j, a],
            recv_sem=post_recv.at[j, a],
            device_id=partner,
            device_id_type=MESH,
        )

    def start_local(j, carry):
        for a in range(4):
            local_copy(a, j).start()
        return carry

    lax.fori_loop(0, heads, start_local, 0)

    barrier = pltpu.get_barrier_semaphore()

    def greet(device):
        pl.semaphore_signal(barrier, inc=1, device_id=device, device_id_type=MESH)

    greet(partner)
    for d in range(1, views):
        greet({"view": source(d)})
    for by in range(1, RUN + 1):
        greet(at_frame(frame + by))
        greet(at_frame(frame - by))
    pl.semaphore_wait(barrier, views + 2 * RUN)

    def start_pair(j):
        pre_copy(1, j).start()
        pre_copy(2, j).start()

    def start_queries(j):
        pre_copy(0, j).start()
        pre_copy(3, j).start()

    for j in range(min(EARLY, heads)):
        start_pair(j)
    for j in range(min(EARLY - QUERIES_BEHIND, heads)):
        start_queries(j)

    @pl.when(frame == 0)
    def _():
        kv_buf[:, :, :, tokens : 2 * tokens, :] = jnp.zeros(
            (heads, 2, 2, tokens, HEAD_DIM), BF16
        )

    @pl.when(frame == frames - 1)
    def _():
        later[...] = jnp.zeros(later.shape, BF16)

    def gather(j):
        for a in (1, 2):
            local_copy(a, j).wait()
            pre_arrival(a, j).wait_recv()

        send_frame(j)

        for side in range(2):
            for band in range(2):
                for row in range(tile_rows):
                    pick[side, band * tile_rows + row] = kv_buf[
                        j, side, band, row * columns : (row + 1) * columns, :
                    ]
        for d in range(1, views):
            for band in range(2):
                row = epi[requester(d), 0, band, d - 1]
                for side in range(2):
                    line_buf[j, side, band, (d - 1) * columns : d * columns, :] = pick[side, row]
            line_copy(d, j).start()

        @pl.when(j < heads - EARLY)
        def _():
            start_pair(j + EARLY)

        @pl.when(j < heads - EARLY + QUERIES_BEHIND)
        def _():
            start_queries(j + EARLY - QUERIES_BEHIND)

    first_row = lax.broadcasted_iota(jnp.int32, (set_size, 1), 0)
    masked = (first_row >= tokens) & (first_row < 2 * tokens) & (frame == 0)
    bias = jnp.where(masked, -1e30, 0.0).astype(F32)

    def attend(j, band):
        queries = q_buf[j, band]
        grads = g_buf[j, band]
        keys = kv_buf[j, 0, band]
        values = kv_buf[j, 1, band]
        scores = dot(keys, queries, 1, 1) * scale + bias
        weights = jnp.exp(scores - jnp.max(scores, axis=0, keepdims=True))
        probs = weights * (1.0 / jnp.sum(weights, axis=0, keepdims=True))
        probs_low = probs.astype(BF16)
        attended = dot(values, probs_low, 0, 0).astype(BF16)
        results[0, j, band] = attended.astype(F32).T.astype(BF16)
        delta = jnp.sum(
            grads.astype(F32).T * attended.astype(F32), axis=0, keepdims=True
        )
        dprobs = dot(values, grads, 1, 1)
        dscores = (probs * (dprobs - delta)).astype(BF16)
        dq = dot(keys, dscores, 0, 0) * scale
        results[1, j, band] = dq.T.astype(BF16)
        dk = dot(dscores, queries, 1, 0) * scale
        dv = dot(probs_low, grads, 1, 0)
        for side, term in ((0, dk), (1, dv)):
            own[j, side, band] = term[:tokens]
            terms[j, side, band] = term[tokens:].astype(BF16)

    def compute(j):
        for a in (0, 3):
            local_copy(a, j).wait()
            pre_arrival(a, j).wait_recv()

        @pl.when(frame > 0)
        def _():
            for p in range(RUN):
                frame_copy(p, j).wait_recv()

        for d in range(1, views):
            line_copy(d, j).wait_recv()

        def one_band(band, carry):
            attend(j, band)
            return carry

        lax.fori_loop(0, 2, one_band, 0)

        send_later(j)

        for d in range(1, views):
            back_copy(d, j).start()
        for a in range(2):
            post_copy(a, j).start()
            out_copy(a, j).start()

    def settle(j):
        @pl.when(frame < frames - 1)
        def _():
            for p in range(RUN):
                later_copy(p, j).wait_recv()

        for d in range(1, views):
            back_copy(d, j).wait_recv()

        step = 16
        chunks = columns // step

        def chunk(i, carry):
            side = i // chunks
            at = pl.multiple_of((i % chunks) * step, step)
            sums = []
            for row in range(2 * tile_rows):
                here = pl.ds((row % tile_rows) * columns + at, step)
                band = row // tile_rows
                sums.append(own[j, side, band, here, :] + later[j, side, band, here, :].astype(F32))
            for d in range(1, views):
                for band in range(2):
                    slot = back[j, side, band, pl.ds((d - 1) * columns + at, step), :].astype(F32)
                    for row in range(2 * tile_rows):
                        sums[row] += slot * holds[band, d - 1, row]
            for row in range(2 * tile_rows):
                here = pl.ds((row % tile_rows) * columns + at, step)
                results[2 + side, j, row // tile_rows, here, :] = sums[row].astype(BF16)
            return carry

        lax.fori_loop(0, 2 * chunks, chunk, 0)
        for a in range(2, 4):
            post_copy(a, j).start()
            out_copy(a, j).start()

    def stage(t, carry):
        def at_stage(lag, step):
            @pl.when((t >= lag) & (t < heads + lag))
            def _():
                step(t - lag)

        at_stage(0, gather)
        at_stage(LAG_COMPUTE, compute)
        at_stage(LAG_AHEAD, pass_ahead)
        at_stage(LAG_SETTLE, settle)
        at_stage(LAG_BEHIND, pass_behind)
        return carry

    lax.fori_loop(0, heads + LAG_SETTLE, stage, 0)

    def drain(j, carry):
        for a in range(4):
            pre_copy(a, j).wait_send()

        @pl.when(frame < frames - 1)
        def _():
            for p in range(RUN):
                frame_copy(p, j).wait_send()

        @pl.when(frame > 0)
        def _():
            for p in range(RUN):
                later_copy(p, j).wait_send()

        @pl.when(passes_ahead)
        def _():
            ahead_pass(j).wait_send()

        @pl.when(passes_behind & (j < RELAYED))
        def _():
            behind_pass(j).wait_send()

        for d in range(1, views):
            line_copy(d, j).wait_send()
            back_copy(d, j).wait_send()
        for a in range(4):
            post_copy(a, j).wait_send()
            post_arrival(a, j).wait_recv()
            out_copy(a, j).wait()
        return carry

    lax.fori_loop(0, heads, drain, 0)


def body(query_vectors, key_vectors, value_vectors, out_grad, epi_rows):
    views = lax.axis_size("view")
    frames = lax.axis_size("tm")
    bands = lax.axis_size("height")
    shape = query_vectors.shape
    tile_rows, columns, features = shape[2:]
    tokens = tile_rows * columns
    heads = features // HEAD_DIM // bands
    others = views - 1
    set_size = 2 * tokens + others * columns
    flat = [x.reshape(tokens, features) for x in (query_vectors, key_vectors, value_vectors, out_grad)]
    viewers = jnp.arange(views, dtype=jnp.int32)
    theirs = (lax.axis_index("view") - viewers) % views
    asked = theirs[:, None] == jnp.arange(1, views, dtype=jnp.int32)[None, :]
    rows = jnp.sum(epi_rows[:, 0] * asked[:, None, :], axis=0)
    holds = (rows[:, :, None] == jnp.arange(bands * tile_rows, dtype=jnp.int32)).astype(F32)
    dma = pltpu.SemaphoreType.DMA
    outs = pl.pallas_call(
        functools.partial(kernel, views, frames, columns, tile_rows, heads),
        out_shape=[jax.ShapeDtypeStruct((tokens, features), BF16)] * 4,
        in_specs=[pl.BlockSpec(memory_space=pl.ANY)] * 4 + [pl.BlockSpec(memory_space=pltpu.SMEM)] * 2,
        out_specs=[pl.BlockSpec(memory_space=pl.ANY)] * 4,
        scratch_shapes=[
            pltpu.VMEM((heads, 2, tokens, HEAD_DIM), BF16),
            pltpu.VMEM((heads, 2, tokens, HEAD_DIM), BF16),
            pltpu.VMEM((heads, 2, 2, set_size, HEAD_DIM), BF16),
            pltpu.VMEM((heads, 2, 2, others * columns, HEAD_DIM), BF16),
            pltpu.VMEM((2, 2 * tile_rows, columns, HEAD_DIM), BF16),
            pltpu.VMEM((heads, 2, 2, set_size - tokens, HEAD_DIM), BF16),
            pltpu.VMEM((heads, 2, 2, tokens, HEAD_DIM), F32),
            pltpu.VMEM((heads, 2, 2, tokens, HEAD_DIM), BF16),
            pltpu.VMEM((heads, 2, 2, others * columns, HEAD_DIM), BF16),
            pltpu.VMEM((4, heads, 2, tokens, HEAD_DIM), BF16),
            pltpu.VMEM((heads, tokens, HEAD_DIM), BF16),
            pltpu.VMEM((heads, tokens, HEAD_DIM), BF16),
            dma((heads, 4)),
            dma((heads, 4)),
            dma((heads, 4)),
            dma((heads, RUN)),
            dma((heads, RUN)),
            dma((heads, others)),
            dma((heads, others)),
            dma((heads, RUN)),
            dma((heads, RUN)),
            dma((heads,)),
            dma((heads,)),
            dma((heads,)),
            dma((heads,)),
            dma((heads, others)),
            dma((heads, others)),
            dma((heads, 4)),
            dma((heads, 4)),
            dma((heads, 4)),
        ],
        compiler_params=pltpu.CompilerParams(
            collective_id=0, has_side_effects=True, vmem_limit_bytes=52 * 1024 * 1024
        ),
        name="attention",
    )(*flat, epi_rows, holds)
    return tuple(x.reshape(shape) for x in outs)


def solution(mesh):
    tiled = P("view", "tm", "height", None, None)
    return jax.shard_map(
        body,
        mesh=mesh,
        in_specs=(tiled, tiled, tiled, tiled, P(None, "tm", None, None)),
        out_specs=(tiled, tiled, tiled, tiled),
        check_vma=False,
    )
```

```python
import functools

import jax
import jax.numpy as jnp
from jax import lax
from jax.experimental import pallas as pl
from jax.experimental.pallas import tpu as pltpu
from jax.sharding import PartitionSpec as P

HEAD_DIM = 128
RUN = 4
RELAYED = 5
EARLY = 3
QUERIES_BEHIND = 2
LAG_AHEAD = 0
LAG_COMPUTE = 3
LAG_BEHIND = 3
LAG_SETTLE = 4
MESH = pl.DeviceIdType.MESH
F32 = jnp.float32
BF16 = jnp.bfloat16


def dot(a, b, over_a, over_b):
    return lax.dot_general(a, b, (((over_a,), (over_b,)), ((), ())), preferred_element_type=F32)


def kernel(
    views, frames, columns, tile_rows, heads,
    q_in, k_in, v_in, g_in, epi_in, o_out, dq_out, dk_out, dv_out,
    q_buf, g_buf, kv_buf, line_buf, pick, terms, own, later, back, results, ahead, behind, epi, epi_sem,
    local_sem, pre_send, pre_recv, frame_send, frame_recv, line_send, line_recv,
    later_send, later_recv, ahead_send, ahead_recv, behind_send, behind_recv, back_send, back_recv, post_send, post_recv, out_sem,
):
    view = lax.axis_index("view")
    frame = lax.axis_index("tm")
    height = lax.axis_index("height")
    other = 1 - height
    tokens = tile_rows * columns
    others = views - 1
    set_size = 2 * tokens + others * columns
    scale = HEAD_DIM ** (-0.5)
    inputs = (q_in, k_in, v_in, g_in)
    outputs = (o_out, dq_out, dk_out, dv_out)
    partner = {"height": other}

    def requester(d):
        return lax.rem(view - d + views, views)

    def source(d):
        return lax.rem(view + d, views)

    def cols(group, j):
        return pl.ds(pl.multiple_of((group * heads + j) * HEAD_DIM, HEAD_DIM), HEAD_DIM)

    def landing(a, j, band):
        if a == 0:
            return q_buf.at[j, band]
        if a == 3:
            return g_buf.at[j, band]
        return kv_buf.at[j, a - 1, band, pl.ds(0, tokens)]

    def local_copy(a, j):
        return pltpu.make_async_copy(
            inputs[a].at[:, cols(height, j)], landing(a, j, height), local_sem.at[j, a]
        )

    def pre_copy(a, j):
        return pltpu.make_async_remote_copy(
            src_ref=inputs[a].at[:, cols(other, j)],
            dst_ref=landing(a, j, height),
            send_sem=pre_send.at[j, a],
            recv_sem=pre_recv.at[j, a],
            device_id=partner,
            device_id_type=MESH,
        )

    def pre_arrival(a, j):
        return pltpu.make_async_remote_copy(
            src_ref=inputs[a].at[:, cols(other, j)],
            dst_ref=landing(a, j, other),
            send_sem=pre_send.at[j, a],
            recv_sem=pre_recv.at[j, a],
            device_id=partner,
            device_id_type=MESH,
        )

    run_at = lax.rem(frame, RUN)
    run_start = frame - run_at

    def at_frame(f):
        return {"tm": lax.rem(f + frames, frames)}

    def remote(src, dst, send_sem, recv_sem, device):
        return pltpu.make_async_remote_copy(
            src_ref=src,
            dst_ref=dst,
            send_sem=send_sem,
            recv_sem=recv_sem,
            device_id=device,
            device_id_type=MESH,
        )

    def earlier_slot(p, j):
        return kv_buf.at[j, p // 2, p % 2, pl.ds(tokens, tokens)]

    def frame_copy(p, j):
        return remote(
            kv_buf.at[j, p // 2, p % 2, pl.ds(0, tokens)],
            earlier_slot(p, j),
            frame_send.at[j, p],
            frame_recv.at[j, p],
            at_frame(frame + 1),
        )

    def ahead_copy(p, j):
        return remote(
            kv_buf.at[j, p // 2, p % 2, pl.ds(0, tokens)],
            ahead.at[j],
            frame_send.at[j, p],
            ahead_recv.at[j],
            at_frame(run_start + p),
        )

    def ahead_pass(j):
        return remote(
            ahead.at[j],
            earlier_slot(run_at, j),
            ahead_send.at[j],
            frame_recv.at[j, run_at],
            at_frame(run_start + RUN),
        )

    def later_copy(p, j):
        return remote(
            terms.at[j, p // 2, p % 2, pl.ds(0, tokens)],
            later.at[j, p // 2, p % 2],
            later_send.at[j, p],
            later_recv.at[j, p],
            at_frame(frame - 1),
        )

    def behind_copy(p, j):
        return remote(
            terms.at[j, p // 2, p % 2, pl.ds(0, tokens)],
            behind.at[j],
            later_send.at[j, p],
            behind_recv.at[j],
            at_frame(run_start + p),
        )

    def behind_pass(j):
        return remote(
            behind.at[j],
            later.at[j, run_at // 2, run_at % 2],
            behind_send.at[j],
            later_recv.at[j, run_at],
            at_frame(run_start - 1),
        )

    passes_ahead = (run_at < RUN - 1) & (frame < frames - RUN)
    passes_behind = (run_at > 0) & (frame >= RUN)

    def send_frame(j):
        @pl.when(run_at < RUN - 1)
        def _():
            for p in range(RUN):
                frame_copy(p, j).start()

        @pl.when((run_at == RUN - 1) & (frame < frames - 1))
        def _():
            frame_copy(RUN - 1, j).start()
            for p in range(RUN - 1):
                ahead_copy(p, j).start()

    def send_later(j):
        @pl.when(run_at > 0)
        def _():
            for p in range(RUN):
                later_copy(p, j).start()

        @pl.when((run_at == 0) & (frame > 0) & (j < RELAYED))
        def _():
            later_copy(0, j).start()
            for p in range(1, RUN):
                behind_copy(p, j).start()

        @pl.when((run_at == 0) & (frame > 0) & (j >= RELAYED))
        def _():
            for p in range(RUN):
                later_copy(p, j).start()

    def pass_ahead(j):
        @pl.when(passes_ahead)
        def _():
            remote(
                ahead.at[j], ahead.at[j], ahead_send.at[j], ahead_recv.at[j], at_frame(run_start + RUN)
            ).wait_recv()
            ahead_pass(j).start()

    def pass_behind(j):
        @pl.when(passes_behind & (j < RELAYED))
        def _():
            remote(
                behind.at[j], behind.at[j], behind_send.at[j], behind_recv.at[j], at_frame(run_start - 1)
            ).wait_recv()
            behind_pass(j).start()

    def line_copy(d, j):
        at = (d - 1) * columns
        return pltpu.make_async_remote_copy(
            src_ref=line_buf.at[j, :, :, pl.ds(at, columns)],
            dst_ref=kv_buf.at[j, :, :, pl.ds(2 * tokens + at, columns)],
            send_sem=line_send.at[j, d - 1],
            recv_sem=line_recv.at[j, d - 1],
            device_id={"view": requester(d)},
            device_id_type=MESH,
        )

    def back_copy(d, j):
        at = (d - 1) * columns
        return pltpu.make_async_remote_copy(
            src_ref=terms.at[j, :, :, pl.ds(tokens + at, columns)],
            dst_ref=back.at[j, :, :, pl.ds(at, columns)],
            send_sem=back_send.at[j, d - 1],
            recv_sem=back_recv.at[j, d - 1],
            device_id={"view": source(d)},
            device_id_type=MESH,
        )

    def out_copy(a, j):
        return pltpu.make_async_copy(
            results.at[a, j, height], outputs[a].at[:, cols(height, j)], out_sem.at[j, a]
        )

    def post_copy(a, j):
        return pltpu.make_async_remote_copy(
            src_ref=results.at[a, j, other],
            dst_ref=outputs[a].at[:, cols(height, j)],
            send_sem=post_send.at[j, a],
            recv_sem=post_recv.at[j, a],
            device_id=partner,
            device_id_type=MESH,
        )

    def post_arrival(a, j):
        return pltpu.make_async_remote_copy(
            src_ref=results.at[a, j, other],
            dst_ref=outputs[a].at[:, cols(other, j)],
            send_sem=post_send.at[j, a],
            recv_sem=post_recv.at[j, a],
            device_id=partner,
            device_id_type=MESH,
        )

    def start_local(j, carry):
        for a in range(4):
            local_copy(a, j).start()
        return carry

    lax.fori_loop(0, heads, start_local, 0)
    rows_copy = pltpu.make_async_copy(epi_in, epi, epi_sem)
    rows_copy.start()

    barrier = pltpu.get_barrier_semaphore()

    def greet(device):
        pl.semaphore_signal(barrier, inc=1, device_id=device, device_id_type=MESH)

    greet(partner)
    for d in range(1, views):
        greet({"view": source(d)})
    for by in range(1, RUN + 1):
        greet(at_frame(frame + by))
        greet(at_frame(frame - by))
    pl.semaphore_wait(barrier, views + 2 * RUN)

    def start_pair(j):
        pre_copy(1, j).start()
        pre_copy(2, j).start()

    def start_queries(j):
        pre_copy(0, j).start()
        pre_copy(3, j).start()

    for j in range(min(EARLY, heads)):
        start_pair(j)
    for j in range(min(EARLY - QUERIES_BEHIND, heads)):
        start_queries(j)

    rows_copy.wait()

    @pl.when(frame == 0)
    def _():
        kv_buf[:, :, :, tokens : 2 * tokens, :] = jnp.zeros(
            (heads, 2, 2, tokens, HEAD_DIM), BF16
        )

    @pl.when(frame == frames - 1)
    def _():
        later[...] = jnp.zeros(later.shape, BF16)

    def gather(j):
        for a in (1, 2):
            local_copy(a, j).wait()
            pre_arrival(a, j).wait_recv()

        send_frame(j)

        for side in range(2):
            for band in range(2):
                for row in range(tile_rows):
                    pick[side, band * tile_rows + row] = kv_buf[
                        j, side, band, row * columns : (row + 1) * columns, :
                    ]
        for d in range(1, views):
            for band in range(2):
                row = epi[0, d - 1, band, requester(d)]
                for side in range(2):
                    line_buf[j, side, band, (d - 1) * columns : d * columns, :] = pick[side, row]
            line_copy(d, j).start()

        @pl.when(j < heads - EARLY)
        def _():
            start_pair(j + EARLY)

        @pl.when(j < heads - EARLY + QUERIES_BEHIND)
        def _():
            start_queries(j + EARLY - QUERIES_BEHIND)

    first_row = lax.broadcasted_iota(jnp.int32, (set_size, 1), 0)
    masked = (first_row >= tokens) & (first_row < 2 * tokens) & (frame == 0)
    bias = jnp.where(masked, -1e30, 0.0).astype(F32)

    def attend(j, band):
        queries = q_buf[j, band]
        grads = g_buf[j, band]
        keys = kv_buf[j, 0, band]
        values = kv_buf[j, 1, band]
        scores = dot(keys, queries, 1, 1) * scale + bias
        weights = jnp.exp(scores - jnp.max(scores, axis=0, keepdims=True))
        probs = weights * (1.0 / jnp.sum(weights, axis=0, keepdims=True))
        probs_low = probs.astype(BF16)
        attended = dot(values, probs_low, 0, 0).astype(BF16)
        results[0, j, band] = attended.astype(F32).T.astype(BF16)
        delta = jnp.sum(
            grads.astype(F32).T * attended.astype(F32), axis=0, keepdims=True
        )
        dprobs = dot(values, grads, 1, 1)
        dscores = (probs * (dprobs - delta)).astype(BF16)
        dq = dot(keys, dscores, 0, 0) * scale
        results[1, j, band] = dq.T.astype(BF16)
        dk = dot(dscores, queries, 1, 0) * scale
        dv = dot(probs_low, grads, 1, 0)
        for side, term in ((0, dk), (1, dv)):
            own[j, side, band] = term[:tokens]
            terms[j, side, band] = term[tokens:].astype(BF16)

    def compute(j):
        for a in (0, 3):
            local_copy(a, j).wait()
            pre_arrival(a, j).wait_recv()

        @pl.when(frame > 0)
        def _():
            for p in range(RUN):
                frame_copy(p, j).wait_recv()

        for d in range(1, views):
            line_copy(d, j).wait_recv()

        def one_band(band, carry):
            attend(j, band)
            return carry

        lax.fori_loop(0, 2, one_band, 0)

        send_later(j)

        for d in range(1, views):
            back_copy(d, j).start()
        for a in range(2):
            post_copy(a, j).start()
            out_copy(a, j).start()

    def settle(j):
        @pl.when(frame < frames - 1)
        def _():
            for p in range(RUN):
                later_copy(p, j).wait_recv()

        for d in range(1, views):
            back_copy(d, j).wait_recv()

        step = 16
        chunks = columns // step

        def chunk(i, carry):
            side = i // chunks
            at = pl.multiple_of((i % chunks) * step, step)
            sums = []
            for row in range(2 * tile_rows):
                here = pl.ds((row % tile_rows) * columns + at, step)
                band = row // tile_rows
                sums.append(own[j, side, band, here, :] + later[j, side, band, here, :].astype(F32))
            for d in range(1, views):
                for band in range(2):
                    row_there = epi[0, d - 1, band, requester(d)]
                    slot = back[j, side, band, pl.ds((d - 1) * columns + at, step), :].astype(F32)
                    for row in range(2 * tile_rows):
                        sums[row] += slot * (row_there == row).astype(F32)
            for row in range(2 * tile_rows):
                here = pl.ds((row % tile_rows) * columns + at, step)
                results[2 + side, j, row // tile_rows, here, :] = sums[row].astype(BF16)
            return carry

        lax.fori_loop(0, 2 * chunks, chunk, 0)
        for a in range(2, 4):
            post_copy(a, j).start()
            out_copy(a, j).start()

    def stage(t, carry):
        def at_stage(lag, step):
            @pl.when((t >= lag) & (t < heads + lag))
            def _():
                step(t - lag)

        at_stage(0, gather)
        at_stage(LAG_COMPUTE, compute)
        at_stage(LAG_AHEAD, pass_ahead)
        at_stage(LAG_SETTLE, settle)
        at_stage(LAG_BEHIND, pass_behind)
        return carry

    lax.fori_loop(0, heads + LAG_SETTLE, stage, 0)

    def drain(j, carry):
        for a in range(4):
            pre_copy(a, j).wait_send()

        @pl.when(frame < frames - 1)
        def _():
            for p in range(RUN):
                frame_copy(p, j).wait_send()

        @pl.when(frame > 0)
        def _():
            for p in range(RUN):
                later_copy(p, j).wait_send()

        @pl.when(passes_ahead)
        def _():
            ahead_pass(j).wait_send()

        @pl.when(passes_behind & (j < RELAYED))
        def _():
            behind_pass(j).wait_send()

        for d in range(1, views):
            line_copy(d, j).wait_send()
            back_copy(d, j).wait_send()
        for a in range(4):
            post_copy(a, j).wait_send()
            post_arrival(a, j).wait_recv()
            out_copy(a, j).wait()
        return carry

    lax.fori_loop(0, heads, drain, 0)


def place(a, b, c, d, a_out, b_out, c_out, d_out, sem):
    part = a.shape[0] // 4
    copies = [
        pltpu.make_async_copy(
            x.at[pl.ds(n * part, part)], y.at[pl.ds(n * part, part)], sem.at[i, n]
        )
        for i, (x, y) in enumerate(((a, a_out), (b, b_out), (c, c_out), (d, d_out)))
        for n in range(4)
    ]
    for copy in copies:
        copy.start()
    for copy in copies:
        copy.wait()


def body(query_vectors, key_vectors, value_vectors, out_grad, epi_rows):
    views = lax.axis_size("view")
    frames = lax.axis_size("tm")
    bands = lax.axis_size("height")
    shape = query_vectors.shape
    tile_rows, columns, features = shape[2:]
    tokens = tile_rows * columns
    heads = features // HEAD_DIM // bands
    others = views - 1
    set_size = 2 * tokens + others * columns
    flat = [x.reshape(tokens, features) for x in (query_vectors, key_vectors, value_vectors, out_grad)]
    dma = pltpu.SemaphoreType.DMA
    outs = pl.pallas_call(
        functools.partial(kernel, views, frames, columns, tile_rows, heads),
        out_shape=[jax.ShapeDtypeStruct((tokens, features), BF16)] * 4,
        in_specs=[pl.BlockSpec(memory_space=pltpu.HBM)] * 5,
        out_specs=[pl.BlockSpec(memory_space=pl.ANY)] * 4,
        scratch_shapes=[
            pltpu.VMEM((heads, 2, tokens, HEAD_DIM), BF16),
            pltpu.VMEM((heads, 2, tokens, HEAD_DIM), BF16),
            pltpu.VMEM((heads, 2, 2, set_size, HEAD_DIM), BF16),
            pltpu.VMEM((heads, 2, 2, others * columns, HEAD_DIM), BF16),
            pltpu.VMEM((2, 2 * tile_rows, columns, HEAD_DIM), BF16),
            pltpu.VMEM((heads, 2, 2, set_size - tokens, HEAD_DIM), BF16),
            pltpu.VMEM((heads, 2, 2, tokens, HEAD_DIM), F32),
            pltpu.VMEM((heads, 2, 2, tokens, HEAD_DIM), BF16),
            pltpu.VMEM((heads, 2, 2, others * columns, HEAD_DIM), BF16),
            pltpu.VMEM((4, heads, 2, tokens, HEAD_DIM), BF16),
            pltpu.VMEM((heads, tokens, HEAD_DIM), BF16),
            pltpu.VMEM((heads, tokens, HEAD_DIM), BF16),
            pltpu.SMEM((1, others, bands, views), jnp.int32),
            dma,
            dma((heads, 4)),
            dma((heads, 4)),
            dma((heads, 4)),
            dma((heads, RUN)),
            dma((heads, RUN)),
            dma((heads, others)),
            dma((heads, others)),
            dma((heads, RUN)),
            dma((heads, RUN)),
            dma((heads,)),
            dma((heads,)),
            dma((heads,)),
            dma((heads,)),
            dma((heads, others)),
            dma((heads, others)),
            dma((heads, 4)),
            dma((heads, 4)),
            dma((heads, 4)),
        ],
        compiler_params=pltpu.CompilerParams(
            collective_id=0, has_side_effects=True, vmem_limit_bytes=101 * 512 * 1024
        ),
        name="attention",
    )(*flat, jnp.transpose(epi_rows, (1, 3, 2, 0)))
    outs = pl.pallas_call(
        place,
        out_shape=[jax.ShapeDtypeStruct((tokens, features), BF16)] * 4,
        in_specs=[pl.BlockSpec(memory_space=pltpu.VMEM)] * 4,
        out_specs=[pl.BlockSpec(memory_space=pltpu.HBM)] * 4,
        scratch_shapes=[dma((4, 4))],
        compiler_params=pltpu.CompilerParams(vmem_limit_bytes=8 * 1024 * 1024),
        name="place",
    )(*outs)
    return tuple(x.reshape(shape) for x in outs)


def solution(mesh):
    tiled = P("view", "tm", "height", None, None)
    return jax.shard_map(
        body,
        mesh=mesh,
        in_specs=(tiled, tiled, tiled, tiled, P(None, "tm", None, None)),
        out_specs=(tiled, tiled, tiled, tiled),
        check_vma=False,
    )
```

```python
import functools

import jax
import jax.numpy as jnp
from jax import lax
from jax.experimental import pallas as pl
from jax.experimental.pallas import tpu as pltpu
from jax.sharding import PartitionSpec as P

HEAD_DIM = 128
RUN = 4
RELAYED = 5
EARLY = 3
QUERIES_BEHIND = 2
LAG_AHEAD = 0
LAG_COMPUTE = 3
LAG_BEHIND = 3
LAG_SETTLE = 4
MESH = pl.DeviceIdType.MESH
F32 = jnp.float32
BF16 = jnp.bfloat16


def dot(a, b, over_a, over_b):
    return lax.dot_general(a, b, (((over_a,), (over_b,)), ((), ())), preferred_element_type=F32)


def kernel(
    views, frames, columns, tile_rows, heads,
    q_in, k_in, v_in, g_in, epi_in, o_out, dq_out, dk_out, dv_out,
    q_buf, g_buf, kv_buf, line_buf, pick, terms, own, later, back, results, ahead, behind, epi, epi_sem,
    local_sem, pre_send, pre_recv, frame_send, frame_recv, line_send, line_recv,
    later_send, later_recv, ahead_send, ahead_recv, behind_send, behind_recv, back_send, back_recv, post_send, post_recv, out_sem,
):
    view = lax.axis_index("view")
    frame = lax.axis_index("tm")
    height = lax.axis_index("height")
    other = 1 - height
    tokens = tile_rows * columns
    others = views - 1
    set_size = 2 * tokens + others * columns
    scale = HEAD_DIM ** (-0.5)
    inputs = (q_in, k_in, v_in, g_in)
    outputs = (o_out, dq_out, dk_out, dv_out)
    partner = {"height": other}

    def requester(d):
        return lax.rem(view - d + views, views)

    def source(d):
        return lax.rem(view + d, views)

    def cols(group, j):
        return pl.ds(pl.multiple_of((group * heads + j) * HEAD_DIM, HEAD_DIM), HEAD_DIM)

    def landing(a, j, band):
        if a == 0:
            return q_buf.at[j, band]
        if a == 3:
            return g_buf.at[j, band]
        return kv_buf.at[j, a - 1, band, pl.ds(0, tokens)]

    def local_copy(a, j):
        return pltpu.make_async_copy(
            inputs[a].at[:, cols(height, j)], landing(a, j, height), local_sem.at[j, a]
        )

    def pre_copy(a, j):
        return pltpu.make_async_remote_copy(
            src_ref=inputs[a].at[:, cols(other, j)],
            dst_ref=landing(a, j, height),
            send_sem=pre_send.at[j, a],
            recv_sem=pre_recv.at[j, a],
            device_id=partner,
            device_id_type=MESH,
        )

    def pre_arrival(a, j):
        return pltpu.make_async_remote_copy(
            src_ref=inputs[a].at[:, cols(other, j)],
            dst_ref=landing(a, j, other),
            send_sem=pre_send.at[j, a],
            recv_sem=pre_recv.at[j, a],
            device_id=partner,
            device_id_type=MESH,
        )

    run_at = lax.rem(frame, RUN)
    run_start = frame - run_at

    def at_frame(f):
        return {"tm": lax.rem(f + frames, frames)}

    def remote(src, dst, send_sem, recv_sem, device):
        return pltpu.make_async_remote_copy(
            src_ref=src,
            dst_ref=dst,
            send_sem=send_sem,
            recv_sem=recv_sem,
            device_id=device,
            device_id_type=MESH,
        )

    def earlier_slot(p, j):
        return kv_buf.at[j, p // 2, p % 2, pl.ds(tokens, tokens)]

    def frame_copy(p, j):
        return remote(
            kv_buf.at[j, p // 2, p % 2, pl.ds(0, tokens)],
            earlier_slot(p, j),
            frame_send.at[j, p],
            frame_recv.at[j, p],
            at_frame(frame + 1),
        )

    def ahead_copy(p, j):
        return remote(
            kv_buf.at[j, p // 2, p % 2, pl.ds(0, tokens)],
            ahead.at[j],
            frame_send.at[j, p],
            ahead_recv.at[j],
            at_frame(run_start + p),
        )

    def ahead_pass(j):
        return remote(
            ahead.at[j],
            earlier_slot(run_at, j),
            ahead_send.at[j],
            frame_recv.at[j, run_at],
            at_frame(run_start + RUN),
        )

    def later_copy(p, j):
        return remote(
            terms.at[j, p // 2, p % 2, pl.ds(0, tokens)],
            later.at[j, p // 2, p % 2],
            later_send.at[j, p],
            later_recv.at[j, p],
            at_frame(frame - 1),
        )

    def behind_copy(p, j):
        return remote(
            terms.at[j, p // 2, p % 2, pl.ds(0, tokens)],
            behind.at[j],
            later_send.at[j, p],
            behind_recv.at[j],
            at_frame(run_start + p),
        )

    def behind_pass(j):
        return remote(
            behind.at[j],
            later.at[j, run_at // 2, run_at % 2],
            behind_send.at[j],
            later_recv.at[j, run_at],
            at_frame(run_start - 1),
        )

    passes_ahead = (run_at < RUN - 1) & (frame < frames - RUN)
    passes_behind = (run_at > 0) & (frame >= RUN)

    def send_frame(j):
        @pl.when(run_at < RUN - 1)
        def _():
            for p in range(RUN):
                frame_copy(p, j).start()

        @pl.when((run_at == RUN - 1) & (frame < frames - 1))
        def _():
            frame_copy(RUN - 1, j).start()
            for p in range(RUN - 1):
                ahead_copy(p, j).start()

    def send_later(j):
        @pl.when(run_at > 0)
        def _():
            for p in range(RUN):
                later_copy(p, j).start()

        @pl.when((run_at == 0) & (frame > 0) & (j < RELAYED))
        def _():
            later_copy(0, j).start()
            for p in range(1, RUN):
                behind_copy(p, j).start()

        @pl.when((run_at == 0) & (frame > 0) & (j >= RELAYED))
        def _():
            for p in range(RUN):
                later_copy(p, j).start()

    def pass_ahead(j):
        @pl.when(passes_ahead)
        def _():
            remote(
                ahead.at[j], ahead.at[j], ahead_send.at[j], ahead_recv.at[j], at_frame(run_start + RUN)
            ).wait_recv()
            ahead_pass(j).start()

    def pass_behind(j):
        @pl.when(passes_behind & (j < RELAYED))
        def _():
            remote(
                behind.at[j], behind.at[j], behind_send.at[j], behind_recv.at[j], at_frame(run_start - 1)
            ).wait_recv()
            behind_pass(j).start()

    def line_copy(d, j):
        at = (d - 1) * columns
        return pltpu.make_async_remote_copy(
            src_ref=line_buf.at[j, :, :, pl.ds(at, columns)],
            dst_ref=kv_buf.at[j, :, :, pl.ds(2 * tokens + at, columns)],
            send_sem=line_send.at[j, d - 1],
            recv_sem=line_recv.at[j, d - 1],
            device_id={"view": requester(d)},
            device_id_type=MESH,
        )

    def back_copy(d, j):
        at = (d - 1) * columns
        return pltpu.make_async_remote_copy(
            src_ref=terms.at[j, :, :, pl.ds(tokens + at, columns)],
            dst_ref=back.at[j, :, :, pl.ds(at, columns)],
            send_sem=back_send.at[j, d - 1],
            recv_sem=back_recv.at[j, d - 1],
            device_id={"view": source(d)},
            device_id_type=MESH,
        )

    def out_copy(a, j):
        return pltpu.make_async_copy(
            results.at[a, j, height], outputs[a].at[:, cols(height, j)], out_sem.at[j, a]
        )

    def post_copy(a, j):
        return pltpu.make_async_remote_copy(
            src_ref=results.at[a, j, other],
            dst_ref=outputs[a].at[:, cols(height, j)],
            send_sem=post_send.at[j, a],
            recv_sem=post_recv.at[j, a],
            device_id=partner,
            device_id_type=MESH,
        )

    def post_arrival(a, j):
        return pltpu.make_async_remote_copy(
            src_ref=results.at[a, j, other],
            dst_ref=outputs[a].at[:, cols(other, j)],
            send_sem=post_send.at[j, a],
            recv_sem=post_recv.at[j, a],
            device_id=partner,
            device_id_type=MESH,
        )

    barrier = pltpu.get_barrier_semaphore()

    def greet(device):
        pl.semaphore_signal(barrier, inc=1, device_id=device, device_id_type=MESH)

    greet(partner)
    for d in range(1, views):
        greet({"view": source(d)})
    for by in range(1, RUN + 1):
        greet(at_frame(frame + by))
        greet(at_frame(frame - by))

    def start_local(j, carry):
        for a in range(4):
            local_copy(a, j).start()
        return carry

    lax.fori_loop(0, heads, start_local, 0)
    rows_copy = pltpu.make_async_copy(epi_in, epi, epi_sem)
    rows_copy.start()

    pl.semaphore_wait(barrier, views + 2 * RUN)

    def start_pair(j):
        pre_copy(1, j).start()
        pre_copy(2, j).start()

    def start_queries(j):
        pre_copy(0, j).start()
        pre_copy(3, j).start()

    for j in range(min(EARLY, heads)):
        start_pair(j)
    for j in range(min(EARLY - QUERIES_BEHIND, heads)):
        start_queries(j)

    rows_copy.wait()

    @pl.when(frame == 0)
    def _():
        kv_buf[:, :, :, tokens : 2 * tokens, :] = jnp.zeros(
            (heads, 2, 2, tokens, HEAD_DIM), BF16
        )

    @pl.when(frame == frames - 1)
    def _():
        later[...] = jnp.zeros(later.shape, BF16)

    def gather(j):
        for a in (1, 2):
            local_copy(a, j).wait()
            pre_arrival(a, j).wait_recv()

        send_frame(j)

        for side in range(2):
            for band in range(2):
                for row in range(tile_rows):
                    pick[side, band * tile_rows + row] = kv_buf[
                        j, side, band, row * columns : (row + 1) * columns, :
                    ]
        for d in range(1, views):
            for band in range(2):
                row = epi[0, d - 1, band, requester(d)]
                for side in range(2):
                    line_buf[j, side, band, (d - 1) * columns : d * columns, :] = pick[side, row]
            line_copy(d, j).start()

        @pl.when(j < heads - EARLY)
        def _():
            start_pair(j + EARLY)

        @pl.when(j < heads - EARLY + QUERIES_BEHIND)
        def _():
            start_queries(j + EARLY - QUERIES_BEHIND)

    first_row = lax.broadcasted_iota(jnp.int32, (set_size, 1), 0)
    masked = (first_row >= tokens) & (first_row < 2 * tokens) & (frame == 0)
    bias = jnp.where(masked, -1e30, 0.0).astype(F32)

    def attend(j, band):
        queries = q_buf[j, band]
        grads = g_buf[j, band]
        keys = kv_buf[j, 0, band]
        values = kv_buf[j, 1, band]
        scores = dot(keys, queries, 1, 1) * scale + bias
        weights = jnp.exp(scores - jnp.max(scores, axis=0, keepdims=True))
        probs = weights * (1.0 / jnp.sum(weights, axis=0, keepdims=True))
        probs_low = probs.astype(BF16)
        attended = dot(values, probs_low, 0, 0).astype(BF16)
        results[0, j, band] = attended.astype(F32).T.astype(BF16)
        delta = jnp.sum(
            grads.astype(F32).T * attended.astype(F32), axis=0, keepdims=True
        )
        dprobs = dot(values, grads, 1, 1)
        dscores = (probs * (dprobs - delta)).astype(BF16)
        dq = dot(keys, dscores, 0, 0) * scale
        results[1, j, band] = dq.T.astype(BF16)
        dk = dot(dscores, queries, 1, 0) * scale
        dv = dot(probs_low, grads, 1, 0)
        for side, term in ((0, dk), (1, dv)):
            own[j, side, band] = term[:tokens]
            terms[j, side, band] = term[tokens:].astype(BF16)

    def compute(j):
        for a in (0, 3):
            local_copy(a, j).wait()
            pre_arrival(a, j).wait_recv()

        @pl.when(frame > 0)
        def _():
            for p in range(RUN):
                frame_copy(p, j).wait_recv()

        for d in range(1, views):
            line_copy(d, j).wait_recv()

        def one_band(band, carry):
            attend(j, band)
            return carry

        lax.fori_loop(0, 2, one_band, 0)

        send_later(j)

        for d in range(1, views):
            back_copy(d, j).start()
        for a in range(2):
            post_copy(a, j).start()
            out_copy(a, j).start()

    def settle(j):
        @pl.when(frame < frames - 1)
        def _():
            for p in range(RUN):
                later_copy(p, j).wait_recv()

        for d in range(1, views):
            back_copy(d, j).wait_recv()

        step = 16
        chunks = columns // step

        def chunk(i, carry):
            side = i // chunks
            at = pl.multiple_of((i % chunks) * step, step)
            sums = []
            for row in range(2 * tile_rows):
                here = pl.ds((row % tile_rows) * columns + at, step)
                band = row // tile_rows
                sums.append(own[j, side, band, here, :] + later[j, side, band, here, :].astype(F32))
            for d in range(1, views):
                for band in range(2):
                    row_there = epi[0, d - 1, band, requester(d)]
                    slot = back[j, side, band, pl.ds((d - 1) * columns + at, step), :].astype(F32)
                    for row in range(2 * tile_rows):
                        sums[row] += slot * (row_there == row).astype(F32)
            for row in range(2 * tile_rows):
                here = pl.ds((row % tile_rows) * columns + at, step)
                results[2 + side, j, row // tile_rows, here, :] = sums[row].astype(BF16)
            return carry

        lax.fori_loop(0, 2 * chunks, chunk, 0)
        for a in range(2, 4):
            post_copy(a, j).start()
            out_copy(a, j).start()

    def stage(t, carry):
        def at_stage(lag, step):
            @pl.when((t >= lag) & (t < heads + lag))
            def _():
                step(t - lag)

        at_stage(0, gather)
        at_stage(LAG_COMPUTE, compute)
        at_stage(LAG_AHEAD, pass_ahead)
        at_stage(LAG_SETTLE, settle)
        at_stage(LAG_BEHIND, pass_behind)
        return carry

    lax.fori_loop(0, heads + LAG_SETTLE, stage, 0)

    def drain(j, carry):
        for a in range(4):
            pre_copy(a, j).wait_send()

        @pl.when(frame < frames - 1)
        def _():
            for p in range(RUN):
                frame_copy(p, j).wait_send()

        @pl.when(frame > 0)
        def _():
            for p in range(RUN):
                later_copy(p, j).wait_send()

        @pl.when(passes_ahead)
        def _():
            ahead_pass(j).wait_send()

        @pl.when(passes_behind & (j < RELAYED))
        def _():
            behind_pass(j).wait_send()

        for d in range(1, views):
            line_copy(d, j).wait_send()
            back_copy(d, j).wait_send()
        for a in range(4):
            post_copy(a, j).wait_send()
            post_arrival(a, j).wait_recv()
            out_copy(a, j).wait()
        return carry

    lax.fori_loop(0, heads, drain, 0)


def place(a, b, c, d, a_out, b_out, c_out, d_out, sem):
    part = a.shape[0] // 4
    copies = [
        pltpu.make_async_copy(
            x.at[pl.ds(n * part, part)], y.at[pl.ds(n * part, part)], sem.at[i, n]
        )
        for i, (x, y) in enumerate(((a, a_out), (b, b_out), (c, c_out), (d, d_out)))
        for n in range(4)
    ]
    for copy in copies:
        copy.start()
    for copy in copies:
        copy.wait()


def body(query_vectors, key_vectors, value_vectors, out_grad, epi_rows):
    views = lax.axis_size("view")
    frames = lax.axis_size("tm")
    bands = lax.axis_size("height")
    shape = query_vectors.shape
    tile_rows, columns, features = shape[2:]
    tokens = tile_rows * columns
    heads = features // HEAD_DIM // bands
    others = views - 1
    set_size = 2 * tokens + others * columns
    flat = [x.reshape(tokens, features) for x in (query_vectors, key_vectors, value_vectors, out_grad)]
    dma = pltpu.SemaphoreType.DMA
    outs = pl.pallas_call(
        functools.partial(kernel, views, frames, columns, tile_rows, heads),
        out_shape=[jax.ShapeDtypeStruct((tokens, features), BF16)] * 4,
        in_specs=[pl.BlockSpec(memory_space=pltpu.HBM)] * 5,
        out_specs=[pl.BlockSpec(memory_space=pl.ANY)] * 4,
        scratch_shapes=[
            pltpu.VMEM((heads, 2, tokens, HEAD_DIM), BF16),
            pltpu.VMEM((heads, 2, tokens, HEAD_DIM), BF16),
            pltpu.VMEM((heads, 2, 2, set_size, HEAD_DIM), BF16),
            pltpu.VMEM((heads, 2, 2, others * columns, HEAD_DIM), BF16),
            pltpu.VMEM((2, 2 * tile_rows, columns, HEAD_DIM), BF16),
            pltpu.VMEM((heads, 2, 2, set_size - tokens, HEAD_DIM), BF16),
            pltpu.VMEM((heads, 2, 2, tokens, HEAD_DIM), F32),
            pltpu.VMEM((heads, 2, 2, tokens, HEAD_DIM), BF16),
            pltpu.VMEM((heads, 2, 2, others * columns, HEAD_DIM), BF16),
            pltpu.VMEM((4, heads, 2, tokens, HEAD_DIM), BF16),
            pltpu.VMEM((heads, tokens, HEAD_DIM), BF16),
            pltpu.VMEM((heads, tokens, HEAD_DIM), BF16),
            pltpu.SMEM((1, others, bands, views), jnp.int32),
            dma,
            dma((heads, 4)),
            dma((heads, 4)),
            dma((heads, 4)),
            dma((heads, RUN)),
            dma((heads, RUN)),
            dma((heads, others)),
            dma((heads, others)),
            dma((heads, RUN)),
            dma((heads, RUN)),
            dma((heads,)),
            dma((heads,)),
            dma((heads,)),
            dma((heads,)),
            dma((heads, others)),
            dma((heads, others)),
            dma((heads, 4)),
            dma((heads, 4)),
            dma((heads, 4)),
        ],
        compiler_params=pltpu.CompilerParams(
            collective_id=0, has_side_effects=True, vmem_limit_bytes=101 * 512 * 1024
        ),
        name="attention",
    )(*flat, jnp.transpose(epi_rows, (1, 3, 2, 0)))
    outs = pl.pallas_call(
        place,
        out_shape=[jax.ShapeDtypeStruct((tokens, features), BF16)] * 4,
        in_specs=[pl.BlockSpec(memory_space=pltpu.VMEM)] * 4,
        out_specs=[pl.BlockSpec(memory_space=pltpu.HBM)] * 4,
        scratch_shapes=[dma((4, 4))],
        compiler_params=pltpu.CompilerParams(vmem_limit_bytes=8 * 1024 * 1024),
        name="place",
    )(*outs)
    return tuple(x.reshape(shape) for x in outs)


def solution(mesh):
    tiled = P("view", "tm", "height", None, None)
    return jax.shard_map(
        body,
        mesh=mesh,
        in_specs=(tiled, tiled, tiled, tiled, P(None, "tm", None, None)),
        out_specs=(tiled, tiled, tiled, tiled),
        check_vma=False,
    )
```

```python
import functools

import jax
import jax.numpy as jnp
from jax import lax
from jax.experimental import pallas as pl
from jax.experimental.pallas import tpu as pltpu
from jax.sharding import PartitionSpec as P

HEAD_DIM = 128
RUN = 4
RELAYED = 5
EARLY = 3
QUERIES_BEHIND = 2
LAG_AHEAD = 0
LAG_COMPUTE = 3
LAG_BEHIND = 3
LAG_SETTLE = 4
MESH = pl.DeviceIdType.MESH
F32 = jnp.float32
BF16 = jnp.bfloat16


def dot(a, b, over_a, over_b):
    return lax.dot_general(a, b, (((over_a,), (over_b,)), ((), ())), preferred_element_type=F32)


def kernel(
    views, frames, columns, tile_rows, heads,
    q_in, k_in, v_in, g_in, epi_in, o_out, dq_out, dk_out, dv_out,
    q_buf, g_buf, kv_buf, line_buf, pick, terms, own, later, back, results, ahead, behind, epi, epi_sem,
    local_sem, pre_send, pre_recv, frame_send, frame_recv, line_send, line_recv,
    later_send, later_recv, ahead_send, ahead_recv, behind_send, behind_recv, back_send, back_recv, post_send, post_recv, out_sem,
):
    view = lax.axis_index("view")
    frame = lax.axis_index("tm")
    height = lax.axis_index("height")
    other = 1 - height
    tokens = tile_rows * columns
    others = views - 1
    set_size = 2 * tokens + others * columns
    scale = HEAD_DIM ** (-0.5)
    inputs = (q_in, k_in, v_in, g_in)
    outputs = (o_out, dq_out, dk_out, dv_out)
    partner = {"height": other}

    def requester(d):
        return lax.rem(view - d + views, views)

    def source(d):
        return lax.rem(view + d, views)

    def cols(group, j):
        return pl.ds(pl.multiple_of((group * heads + j) * HEAD_DIM, HEAD_DIM), HEAD_DIM)

    def landing(a, j, band):
        if a == 0:
            return q_buf.at[j, band]
        if a == 3:
            return g_buf.at[j, band]
        return kv_buf.at[j, a - 1, band, pl.ds(0, tokens)]

    def local_copy(a, j):
        return pltpu.make_async_copy(
            inputs[a].at[:, cols(height, j)], landing(a, j, height), local_sem.at[j, a]
        )

    def pre_copy(a, j):
        return pltpu.make_async_remote_copy(
            src_ref=inputs[a].at[:, cols(other, j)],
            dst_ref=landing(a, j, height),
            send_sem=pre_send.at[j, a],
            recv_sem=pre_recv.at[j, a],
            device_id=partner,
            device_id_type=MESH,
        )

    def pre_arrival(a, j):
        return pltpu.make_async_remote_copy(
            src_ref=inputs[a].at[:, cols(other, j)],
            dst_ref=landing(a, j, other),
            send_sem=pre_send.at[j, a],
            recv_sem=pre_recv.at[j, a],
            device_id=partner,
            device_id_type=MESH,
        )

    run_at = lax.rem(frame, RUN)
    run_start = frame - run_at

    def at_frame(f):
        return {"tm": lax.rem(f + frames, frames)}

    def remote(src, dst, send_sem, recv_sem, device):
        return pltpu.make_async_remote_copy(
            src_ref=src,
            dst_ref=dst,
            send_sem=send_sem,
            recv_sem=recv_sem,
            device_id=device,
            device_id_type=MESH,
        )

    def earlier_slot(p, j):
        return kv_buf.at[j, p // 2, p % 2, pl.ds(tokens, tokens)]

    def frame_copy(p, j):
        return remote(
            kv_buf.at[j, p // 2, p % 2, pl.ds(0, tokens)],
            earlier_slot(p, j),
            frame_send.at[j, p],
            frame_recv.at[j, p],
            at_frame(frame + 1),
        )

    def ahead_copy(p, j):
        return remote(
            kv_buf.at[j, p // 2, p % 2, pl.ds(0, tokens)],
            ahead.at[j],
            frame_send.at[j, p],
            ahead_recv.at[j],
            at_frame(run_start + p),
        )

    def ahead_pass(j):
        return remote(
            ahead.at[j],
            earlier_slot(run_at, j),
            ahead_send.at[j],
            frame_recv.at[j, run_at],
            at_frame(run_start + RUN),
        )

    def later_copy(p, j):
        return remote(
            terms.at[j, p // 2, p % 2, pl.ds(0, tokens)],
            later.at[j, p // 2, p % 2],
            later_send.at[j, p],
            later_recv.at[j, p],
            at_frame(frame - 1),
        )

    def behind_copy(p, j):
        return remote(
            terms.at[j, p // 2, p % 2, pl.ds(0, tokens)],
            behind.at[j],
            later_send.at[j, p],
            behind_recv.at[j],
            at_frame(run_start + p),
        )

    def behind_pass(j):
        return remote(
            behind.at[j],
            later.at[j, run_at // 2, run_at % 2],
            behind_send.at[j],
            later_recv.at[j, run_at],
            at_frame(run_start - 1),
        )

    passes_ahead = (run_at < RUN - 1) & (frame < frames - RUN)
    passes_behind = (run_at > 0) & (frame >= RUN)

    def send_frame(j):
        @pl.when(run_at < RUN - 1)
        def _():
            for p in range(RUN):
                frame_copy(p, j).start()

        @pl.when((run_at == RUN - 1) & (frame < frames - 1))
        def _():
            frame_copy(RUN - 1, j).start()
            for p in range(RUN - 1):
                ahead_copy(p, j).start()

    def send_later(j):
        @pl.when(run_at > 0)
        def _():
            for p in range(RUN):
                later_copy(p, j).start()

        @pl.when((run_at == 0) & (frame > 0) & (j < RELAYED))
        def _():
            later_copy(0, j).start()
            for p in range(1, RUN):
                behind_copy(p, j).start()

        @pl.when((run_at == 0) & (frame > 0) & (j >= RELAYED))
        def _():
            for p in range(RUN):
                later_copy(p, j).start()

    def pass_ahead(j):
        @pl.when(passes_ahead)
        def _():
            remote(
                ahead.at[j], ahead.at[j], ahead_send.at[j], ahead_recv.at[j], at_frame(run_start + RUN)
            ).wait_recv()
            ahead_pass(j).start()

    def pass_behind(j):
        @pl.when(passes_behind & (j < RELAYED))
        def _():
            remote(
                behind.at[j], behind.at[j], behind_send.at[j], behind_recv.at[j], at_frame(run_start - 1)
            ).wait_recv()
            behind_pass(j).start()

    def line_copy(d, j):
        at = (d - 1) * columns
        return pltpu.make_async_remote_copy(
            src_ref=line_buf.at[j, :, :, pl.ds(at, columns)],
            dst_ref=kv_buf.at[j, :, :, pl.ds(2 * tokens + at, columns)],
            send_sem=line_send.at[j, d - 1],
            recv_sem=line_recv.at[j, d - 1],
            device_id={"view": requester(d)},
            device_id_type=MESH,
        )

    def back_copy(d, j):
        at = (d - 1) * columns
        return pltpu.make_async_remote_copy(
            src_ref=terms.at[j, :, :, pl.ds(tokens + at, columns)],
            dst_ref=back.at[j, :, :, pl.ds(at, columns)],
            send_sem=back_send.at[j, d - 1],
            recv_sem=back_recv.at[j, d - 1],
            device_id={"view": source(d)},
            device_id_type=MESH,
        )

    def out_copy(a, j):
        return pltpu.make_async_copy(
            results.at[a, j, height], outputs[a].at[:, cols(height, j)], out_sem.at[j, a]
        )

    def post_copy(a, j):
        return pltpu.make_async_remote_copy(
            src_ref=results.at[a, j, other],
            dst_ref=outputs[a].at[:, cols(height, j)],
            send_sem=post_send.at[j, a],
            recv_sem=post_recv.at[j, a],
            device_id=partner,
            device_id_type=MESH,
        )

    def post_arrival(a, j):
        return pltpu.make_async_remote_copy(
            src_ref=results.at[a, j, other],
            dst_ref=outputs[a].at[:, cols(other, j)],
            send_sem=post_send.at[j, a],
            recv_sem=post_recv.at[j, a],
            device_id=partner,
            device_id_type=MESH,
        )

    barrier = pltpu.get_barrier_semaphore()

    def greet(device):
        pl.semaphore_signal(barrier, inc=1, device_id=device, device_id_type=MESH)

    greet(partner)
    for d in range(1, views):
        greet({"view": source(d)})
    for by in range(1, RUN + 1):
        greet(at_frame(frame + by))
        greet(at_frame(frame - by))

    pl.semaphore_wait(barrier, views + 2 * RUN)

    def start_pair(j):
        pre_copy(1, j).start()
        pre_copy(2, j).start()

    def start_queries(j):
        pre_copy(0, j).start()
        pre_copy(3, j).start()

    for j in range(min(EARLY, heads)):
        start_pair(j)
    for j in range(min(EARLY - QUERIES_BEHIND, heads)):
        start_queries(j)

    def start_local(j, carry):
        for a in range(4):
            local_copy(a, j).start()
        return carry

    lax.fori_loop(0, heads, start_local, 0)
    rows_copy = pltpu.make_async_copy(epi_in, epi, epi_sem)
    rows_copy.start()

    rows_copy.wait()

    @pl.when(frame == 0)
    def _():
        kv_buf[:, :, :, tokens : 2 * tokens, :] = jnp.zeros(
            (heads, 2, 2, tokens, HEAD_DIM), BF16
        )

    @pl.when(frame == frames - 1)
    def _():
        later[...] = jnp.zeros(later.shape, BF16)

    def gather(j):
        for a in (1, 2):
            local_copy(a, j).wait()
            pre_arrival(a, j).wait_recv()

        send_frame(j)

        for side in range(2):
            for band in range(2):
                for row in range(tile_rows):
                    pick[side, band * tile_rows + row] = kv_buf[
                        j, side, band, row * columns : (row + 1) * columns, :
                    ]
        for d in range(1, views):
            for band in range(2):
                row = epi[0, d - 1, band, requester(d)]
                for side in range(2):
                    line_buf[j, side, band, (d - 1) * columns : d * columns, :] = pick[side, row]
            line_copy(d, j).start()

        @pl.when(j < heads - EARLY)
        def _():
            start_pair(j + EARLY)

        @pl.when(j < heads - EARLY + QUERIES_BEHIND)
        def _():
            start_queries(j + EARLY - QUERIES_BEHIND)

    first_row = lax.broadcasted_iota(jnp.int32, (set_size, 1), 0)
    masked = (first_row >= tokens) & (first_row < 2 * tokens) & (frame == 0)
    bias = jnp.where(masked, -1e30, 0.0).astype(F32)

    def attend(j, band):
        queries = q_buf[j, band]
        grads = g_buf[j, band]
        keys = kv_buf[j, 0, band]
        values = kv_buf[j, 1, band]
        scores = dot(keys, queries, 1, 1) * scale + bias
        weights = jnp.exp(scores - jnp.max(scores, axis=0, keepdims=True))
        probs = weights * (1.0 / jnp.sum(weights, axis=0, keepdims=True))
        probs_low = probs.astype(BF16)
        attended = dot(values, probs_low, 0, 0).astype(BF16)
        results[0, j, band] = attended.astype(F32).T.astype(BF16)
        delta = jnp.sum(
            grads.astype(F32).T * attended.astype(F32), axis=0, keepdims=True
        )
        dprobs = dot(values, grads, 1, 1)
        dscores = (probs * (dprobs - delta)).astype(BF16)
        dq = dot(keys, dscores, 0, 0) * scale
        results[1, j, band] = dq.T.astype(BF16)
        dk = dot(dscores, queries, 1, 0) * scale
        dv = dot(probs_low, grads, 1, 0)
        for side, term in ((0, dk), (1, dv)):
            own[j, side, band] = term[:tokens]
            terms[j, side, band] = term[tokens:].astype(BF16)

    def compute(j):
        for a in (0, 3):
            local_copy(a, j).wait()
            pre_arrival(a, j).wait_recv()

        @pl.when(frame > 0)
        def _():
            for p in range(RUN):
                frame_copy(p, j).wait_recv()

        for d in range(1, views):
            line_copy(d, j).wait_recv()

        def one_band(band, carry):
            attend(j, band)
            return carry

        lax.fori_loop(0, 2, one_band, 0)

        send_later(j)

        for d in range(1, views):
            back_copy(d, j).start()
        for a in range(2):
            post_copy(a, j).start()
            out_copy(a, j).start()

    def settle(j):
        @pl.when(frame < frames - 1)
        def _():
            for p in range(RUN):
                later_copy(p, j).wait_recv()

        for d in range(1, views):
            back_copy(d, j).wait_recv()

        step = 16
        chunks = columns // step

        def chunk(i, carry):
            side = i // chunks
            at = pl.multiple_of((i % chunks) * step, step)
            sums = []
            for row in range(2 * tile_rows):
                here = pl.ds((row % tile_rows) * columns + at, step)
                band = row // tile_rows
                sums.append(own[j, side, band, here, :] + later[j, side, band, here, :].astype(F32))
            for d in range(1, views):
                for band in range(2):
                    row_there = epi[0, d - 1, band, requester(d)]
                    slot = back[j, side, band, pl.ds((d - 1) * columns + at, step), :].astype(F32)
                    for row in range(2 * tile_rows):
                        sums[row] += slot * (row_there == row).astype(F32)
            for row in range(2 * tile_rows):
                here = pl.ds((row % tile_rows) * columns + at, step)
                results[2 + side, j, row // tile_rows, here, :] = sums[row].astype(BF16)
            return carry

        lax.fori_loop(0, 2 * chunks, chunk, 0)
        for a in range(2, 4):
            post_copy(a, j).start()
            out_copy(a, j).start()

    def stage(t, carry):
        def at_stage(lag, step):
            @pl.when((t >= lag) & (t < heads + lag))
            def _():
                step(t - lag)

        at_stage(0, gather)
        at_stage(LAG_COMPUTE, compute)
        at_stage(LAG_AHEAD, pass_ahead)
        at_stage(LAG_SETTLE, settle)
        at_stage(LAG_BEHIND, pass_behind)
        return carry

    lax.fori_loop(0, heads + LAG_SETTLE, stage, 0)

    def drain(j, carry):
        for a in range(4):
            pre_copy(a, j).wait_send()

        @pl.when(frame < frames - 1)
        def _():
            for p in range(RUN):
                frame_copy(p, j).wait_send()

        @pl.when(frame > 0)
        def _():
            for p in range(RUN):
                later_copy(p, j).wait_send()

        @pl.when(passes_ahead)
        def _():
            ahead_pass(j).wait_send()

        @pl.when(passes_behind & (j < RELAYED))
        def _():
            behind_pass(j).wait_send()

        for d in range(1, views):
            line_copy(d, j).wait_send()
            back_copy(d, j).wait_send()
        for a in range(4):
            post_copy(a, j).wait_send()
            post_arrival(a, j).wait_recv()
            out_copy(a, j).wait()
        return carry

    lax.fori_loop(0, heads, drain, 0)


def place(a, b, c, d, a_out, b_out, c_out, d_out, sem):
    part = a.shape[0] // 4
    copies = [
        pltpu.make_async_copy(
            x.at[pl.ds(n * part, part)], y.at[pl.ds(n * part, part)], sem.at[i, n]
        )
        for i, (x, y) in enumerate(((a, a_out), (b, b_out), (c, c_out), (d, d_out)))
        for n in range(4)
    ]
    for copy in copies:
        copy.start()
    for copy in copies:
        copy.wait()


def body(query_vectors, key_vectors, value_vectors, out_grad, epi_rows):
    views = lax.axis_size("view")
    frames = lax.axis_size("tm")
    bands = lax.axis_size("height")
    shape = query_vectors.shape
    tile_rows, columns, features = shape[2:]
    tokens = tile_rows * columns
    heads = features // HEAD_DIM // bands
    others = views - 1
    set_size = 2 * tokens + others * columns
    flat = [x.reshape(tokens, features) for x in (query_vectors, key_vectors, value_vectors, out_grad)]
    dma = pltpu.SemaphoreType.DMA
    outs = pl.pallas_call(
        functools.partial(kernel, views, frames, columns, tile_rows, heads),
        out_shape=[jax.ShapeDtypeStruct((tokens, features), BF16)] * 4,
        in_specs=[pl.BlockSpec(memory_space=pltpu.HBM)] * 5,
        out_specs=[pl.BlockSpec(memory_space=pl.ANY)] * 4,
        scratch_shapes=[
            pltpu.VMEM((heads, 2, tokens, HEAD_DIM), BF16),
            pltpu.VMEM((heads, 2, tokens, HEAD_DIM), BF16),
            pltpu.VMEM((heads, 2, 2, set_size, HEAD_DIM), BF16),
            pltpu.VMEM((heads, 2, 2, others * columns, HEAD_DIM), BF16),
            pltpu.VMEM((2, 2 * tile_rows, columns, HEAD_DIM), BF16),
            pltpu.VMEM((heads, 2, 2, set_size - tokens, HEAD_DIM), BF16),
            pltpu.VMEM((heads, 2, 2, tokens, HEAD_DIM), F32),
            pltpu.VMEM((heads, 2, 2, tokens, HEAD_DIM), BF16),
            pltpu.VMEM((heads, 2, 2, others * columns, HEAD_DIM), BF16),
            pltpu.VMEM((4, heads, 2, tokens, HEAD_DIM), BF16),
            pltpu.VMEM((heads, tokens, HEAD_DIM), BF16),
            pltpu.VMEM((heads, tokens, HEAD_DIM), BF16),
            pltpu.SMEM((1, others, bands, views), jnp.int32),
            dma,
            dma((heads, 4)),
            dma((heads, 4)),
            dma((heads, 4)),
            dma((heads, RUN)),
            dma((heads, RUN)),
            dma((heads, others)),
            dma((heads, others)),
            dma((heads, RUN)),
            dma((heads, RUN)),
            dma((heads,)),
            dma((heads,)),
            dma((heads,)),
            dma((heads,)),
            dma((heads, others)),
            dma((heads, others)),
            dma((heads, 4)),
            dma((heads, 4)),
            dma((heads, 4)),
        ],
        compiler_params=pltpu.CompilerParams(
            collective_id=0, has_side_effects=True, vmem_limit_bytes=101 * 512 * 1024
        ),
        name="attention",
    )(*flat, jnp.transpose(epi_rows, (1, 3, 2, 0)))
    outs = pl.pallas_call(
        place,
        out_shape=[jax.ShapeDtypeStruct((tokens, features), BF16)] * 4,
        in_specs=[pl.BlockSpec(memory_space=pltpu.VMEM)] * 4,
        out_specs=[pl.BlockSpec(memory_space=pltpu.HBM)] * 4,
        scratch_shapes=[dma((4, 4))],
        compiler_params=pltpu.CompilerParams(vmem_limit_bytes=8 * 1024 * 1024),
        name="place",
    )(*outs)
    return tuple(x.reshape(shape) for x in outs)


def solution(mesh):
    tiled = P("view", "tm", "height", None, None)
    return jax.shard_map(
        body,
        mesh=mesh,
        in_specs=(tiled, tiled, tiled, tiled, P(None, "tm", None, None)),
        out_specs=(tiled, tiled, tiled, tiled),
        check_vma=False,
    )
```
